32 devices in a mesh: parts: 2 (over x), row: 2 (over core), col: 8 (over z, y).
Axes of the slice: x: 2, y: 2, z: 4, core: 2. Of those that a mesh axis runs over, the one named last changes fastest.
Arguments:
- points: bfloat16 [16384, 128], P(('parts', 'row', 'col')), parts along dimension 0, may hold values from -4 to 4
- vectors: bfloat16 [16384, 64], P(('parts', 'row', 'col')), parts along dimension 0, may hold values from -18 to 18
Outputs:
- smoothed: float32 [16384, 64], P(('parts', 'row', 'col')), parts along dimension 0
- log_density: float32 [16384], P(('parts', 'row', 'col')), parts along dimension 0
The draws below stay inside these ranges and needn't reach their ends.
There are 2 independent parts, one for each index of `parts`. The reference program is written for one: setup_inputs(seed, part) draws one part's arguments, and reference() takes and returns one part's arrays. A program takes and returns all parts, laid end to end along the dimension named above; each array names one. Nothing has to cross between parts.
All inputs are finite; a program needn't handle non-finite values.
Results may differ from the reference program's by a relative error of at most 0.0029.
Values may be sent and summed in bfloat16 or wider, within the bound.
No kernel may reach another device: no remote copies, remote signals or barrier semaphores. Data moves between devices by JAX's collectives and lax.ppermute only.
A program may use at most 64 MiB of HBM per device.

```python
import math
import jax
import jax.numpy as jnp
from jax import lax

F = 128
W = 64
NPTS = 8192


def draw_points(key, part):
    key_main = jax.random.fold_in(key, 11)
    values = jax.random.truncated_normal(key_main, -4.0, 4.0, (NPTS, F), jnp.float32)
    return values.astype(jnp.bfloat16)


def level_of(rng, extent, pieces, least, high):
    gain, own = 1.0, jax.random.fold_in(rng, 6)
    for position, shards_of in pieces:
        steps = jnp.exp(jax.random.uniform(jax.random.fold_in(own, position), (shards_of,), jnp.float32, least / len(pieces), high / len(pieces)))
        gain = gain * jnp.repeat(steps, extent[position] // shards_of).reshape([-1 if axis == position else 1 for axis in range(len(extent))])
    return gain


def bell_draw(own_key, shape, deviation, bound, split=(), kind=jnp.bfloat16):
    drawn = deviation * jax.random.normal(own_key, shape, jnp.float32)
    if split:
        drawn = drawn * level_of(own_key, shape, split, -0.22, 0.18)
    return jnp.clip(drawn, -bound, bound).astype(kind)


def setup_inputs(seed: int = 0, part: int = 0) -> dict:
    arg_keys = jax.random.split(jax.random.key(seed), 3)
    part_splits = jax.random.split(jax.random.fold_in(arg_keys[2], part), 3)
    return {
        "points": draw_points(jax.random.fold_in(jax.random.fold_in(arg_keys[2], part), 71), part),
        "vectors": bell_draw(part_splits[1], (NPTS, W), 3.0, 18.0, ((0, 16),)),
    }


def reference(points, vectors):
    npts = points.shape[0]
    feats = points.shape[1]
    width = 1.05 * math.sqrt(feats)
    norms = lax.optimization_barrier(jnp.sum(points.astype(jnp.float32) ** 2, axis=1))
    ids = jnp.arange(npts, dtype=jnp.int32)
    size = 512 if npts % 512 == 0 else npts
    starts = jnp.arange(npts // size, dtype=jnp.int32) * size

    def kernel_rows(start):
        block = lax.dynamic_slice_in_dim(points, start, size, 0)
        block_norms = lax.dynamic_slice_in_dim(norms, start, size, 0)
        cross = jnp.dot(block, points.T, preferred_element_type=jnp.float32)
        dist = block_norms[:, None] + norms[None, :] - 2.0 * cross
        values = jnp.exp((2.0 * feats - dist) / width)
        rows = start + jnp.arange(size, dtype=jnp.int32)
        return jnp.where(rows[:, None] == ids[None, :], jnp.zeros_like(values), values)
    sums = lax.map(lambda start: lax.optimization_barrier(jnp.sum(kernel_rows(start), axis=1)), starts).reshape(npts)
    density = sums / npts

    def product_rows(start):
        weight = kernel_rows(start) / density[None, :]
        degree = lax.optimization_barrier(jnp.sum(weight, axis=1))
        numer = jnp.dot(weight.astype(jnp.bfloat16), vectors, preferred_element_type=jnp.float32)
        return numer / degree[:, None]
    smoothed = lax.map(product_rows, starts).reshape(npts, vectors.shape[1])
    return (smoothed, jnp.log(density))
```

```python
import functools
import math

import jax
import jax.numpy as jnp
from jax import lax
from jax.experimental import pallas as pl
from jax.experimental.pallas import tpu as pltpu
from jax.sharding import PartitionSpec as P

MIB = 2**20
NT = (((1,), (1,)), ((), ()))
VMEM_SPEC = pl.BlockSpec(memory_space=pltpu.VMEM)


def by_blocks(piece, tile_fn):
    count = piece.shape[0]
    size = 512
    groups = piece.reshape(count // size, size, piece.shape[1])
    firsts = jnp.arange(count // size, dtype=jnp.int32) * size
    return lax.map(lambda item: tile_fn(item[0], item[1]), (groups, firsts))


def plain_device(points, vectors):
    rows_dev = points.shape[0]
    feats = points.shape[1]
    n_col = lax.axis_size("col")
    n_row = lax.axis_size("row")
    half = rows_dev * n_col
    total_pts = half * n_row
    row_pos = lax.axis_index("row")
    col_pos = lax.axis_index("col")
    width = 1.05 * math.sqrt(feats)
    col_points = lax.all_gather(points, "row", axis=0, tiled=True)
    col_vectors = lax.all_gather(vectors, "row", axis=0, tiled=True)
    local = jnp.arange(n_row * rows_dev, dtype=jnp.int32)
    col_ids = local // rows_dev * half + col_pos * rows_dev + local % rows_dev
    col_norms = jnp.sum(col_points.astype(jnp.float32) ** 2, axis=1)
    row_base = row_pos * half
    piece = lax.all_gather(points, "col", axis=0, tiled=True)

    def kernel_tile(block, first):
        norms = jnp.sum(block.astype(jnp.float32) ** 2, axis=1)
        cross = lax.dot_general(block, col_points, NT, preferred_element_type=jnp.float32)
        dist = norms[:, None] + col_norms[None, :] - 2.0 * cross
        values = jnp.exp((2.0 * feats - dist) / width)
        rows = row_base + first + jnp.arange(block.shape[0], dtype=jnp.int32)
        return jnp.where(rows[:, None] == col_ids[None, :], jnp.zeros_like(values), values)

    sums = by_blocks(piece, lambda block, first: jnp.sum(kernel_tile(block, first), axis=1))
    own_sums = lax.psum_scatter(sums.reshape(-1), "col", scatter_dimension=0, tiled=True)
    own_density = own_sums / total_pts
    col_density = lax.all_gather(own_density, "row", axis=0, tiled=True)

    def product_tile(block, first):
        weight = kernel_tile(block, first) / col_density[None, :]
        degree = jnp.sum(weight, axis=1)
        numer = jnp.dot(
            weight.astype(jnp.bfloat16), col_vectors, preferred_element_type=jnp.float32
        )
        return (numer, degree)

    numer, degree = by_blocks(piece, product_tile)
    numer = numer.reshape(piece.shape[0], vectors.shape[1])
    numer_own = lax.psum_scatter(numer, "col", scatter_dimension=0, tiled=True)
    degree_own = lax.psum_scatter(
        degree.reshape(-1), "col", scatter_dimension=0, tiled=True
    )
    return (numer_own / degree_own[:, None], jnp.log(own_density))


def augment(dst, base, pts, first):
    count, feats = pts.shape
    square = pts.astype(jnp.float32)
    square = square * square
    high = square.astype(jnp.bfloat16)
    low = (square - high.astype(jnp.float32)).astype(jnp.bfloat16)
    pair = jnp.concatenate([high, low], axis=1)
    norm = jnp.dot(
        pair, jnp.ones((2 * feats, 128), jnp.bfloat16), preferred_element_type=jnp.float32
    )
    q = 0.5 * feats - 0.5 * norm
    q0 = q.astype(jnp.bfloat16).astype(jnp.float32)
    rest = q - q0
    q1 = rest.astype(jnp.bfloat16).astype(jnp.float32)
    q2 = rest - q1
    lane = lax.broadcasted_iota(jnp.int32, (count, 128), 1)
    other = 3 - first
    extra = jnp.where((lane >= other) & (lane < other + 3), 1.0, 0.0)
    extra = jnp.where(lane == first + 2, q2, extra)
    extra = jnp.where(lane == first + 1, q1, extra)
    extra = jnp.where(lane == first, q0, extra)
    dst[base : base + count, 0:feats] = pts
    dst[base : base + count, feats : feats + 128] = extra.astype(jnp.bfloat16)


def kernel_body(n_rows, n_cols, unit, scale, diagonal, bm, bn, *refs):
    rows = refs[:n_rows]
    cols = refs[n_rows : n_rows + n_cols]
    k_ref, sum_ref, lhs, rhs = refs[n_rows + n_cols :]
    for u in range(n_rows):
        augment(lhs, u * unit, rows[u][...], 0)
    for u in range(n_cols):
        augment(rhs, u * unit, cols[u][...], 3)
    for c0 in range(0, n_cols * unit, bn):
        total = jnp.zeros((8, bn), jnp.float32)
        for r0 in range(0, n_rows * unit, bm):
            half_log = lax.dot_general(
                lhs[r0 : r0 + bm, :],
                rhs[c0 : c0 + bn, :],
                NT,
                preferred_element_type=jnp.float32,
            )
            value = jnp.exp2(half_log * scale)
            if (r0 // unit, c0 // unit) == diagonal:
                i = lax.broadcasted_iota(jnp.int32, (bm, bn), 0) + r0 % unit
                j = lax.broadcasted_iota(jnp.int32, (bm, bn), 1) + c0 % unit
                value = jnp.where(i == j, 0.0, value)
            k_ref[r0 : r0 + bm, c0 : c0 + bn] = value
            total = total + jnp.sum(value.reshape(bm // 8, 8, bn), axis=0)
        sum_ref[0:1, c0 : c0 + bn] = jnp.sum(total, axis=0, keepdims=True)


def kernel_tile(rows, cols, diagonal):
    unit, feats = rows[0].shape
    n_rows, n_cols = len(rows), len(cols)
    scale = 2.0 * math.log2(math.e) / (1.05 * math.sqrt(feats))
    return pl.pallas_call(
        functools.partial(kernel_body, n_rows, n_cols, unit, scale, diagonal, 256, 512),
        out_shape=(
            pltpu.VMEM((n_rows * unit, n_cols * unit), jnp.float32),
            jax.ShapeDtypeStruct((1, n_cols * unit), jnp.float32),
        ),
        in_specs=[VMEM_SPEC] * (n_rows + n_cols),
        out_specs=(VMEM_SPEC, VMEM_SPEC),
        scratch_shapes=[
            pltpu.VMEM((n_rows * unit, feats + 128), jnp.bfloat16),
            pltpu.VMEM((n_cols * unit, feats + 128), jnp.bfloat16),
        ],
        compiler_params=pltpu.CompilerParams(vmem_limit_bytes=20 * MIB),
        name="kernel_tile",
    )(*rows, *cols)


def product_body(n_cols, unit, points_all, bm, k_ref, *refs):
    sums = refs[:n_cols]
    vecs = refs[n_cols : 2 * n_cols]
    keep_ref, give_ref, log_ref, vec_all = refs[2 * n_cols :]
    width = vecs[0].shape[0]
    inverse = []
    for v in range(n_cols):
        total = sums[0][:, v * unit : (v + 1) * unit]
        for u in range(1, n_cols):
            w = v ^ u
            total = total + sums[u][:, w * unit : (w + 1) * unit]
        density = total / points_all
        if v == 0:
            log_ref[...] = jnp.log(density)
        inverse.append(1.0 / density)
        vec_all[0:width, v * unit : (v + 1) * unit] = vecs[v][...]
    inverse = jnp.concatenate(inverse, axis=1)
    ones = lax.broadcasted_iota(jnp.int32, (128 - width, n_cols * unit), 0) == 0
    vec_all[width:128, :] = jnp.where(ones, 1.0, 0.0).astype(jnp.bfloat16)
    for r0 in range(0, k_ref.shape[0], bm):
        weight = (k_ref[r0 : r0 + bm, :] * inverse).astype(jnp.bfloat16)
        numer = lax.dot_general(weight, vec_all[...], NT, preferred_element_type=jnp.float32)
        owner, at = r0 // unit, r0 % unit + r0 // (2 * unit) * unit
        if owner % 2 == 0:
            keep_ref[at : at + bm, :] = numer
        else:
            give_ref[at : at + bm, :] = numer


def product_tile(k, sums, vecs, points_all):
    n_cols = len(sums)
    unit = vecs[0].shape[1]
    shape = jax.ShapeDtypeStruct((k.shape[0] // 2, 128), jnp.float32)
    return pl.pallas_call(
        functools.partial(product_body, n_cols, unit, points_all, 256),
        out_shape=(shape, shape, jax.ShapeDtypeStruct((1, unit), jnp.float32)),
        in_specs=[VMEM_SPEC] * (1 + 2 * n_cols),
        out_specs=(VMEM_SPEC,) * 3,
        scratch_shapes=[pltpu.VMEM((128, n_cols * unit), jnp.bfloat16)],
        compiler_params=pltpu.CompilerParams(vmem_limit_bytes=16 * MIB),
        name="product_tile",
    )(k, *sums, *vecs)


def halves_body(keep_ref, got_ref, own_ref, far_ref):
    unit, height = own_ref.shape[1], own_ref.shape[0]
    own = keep_ref[0:unit, :] + got_ref[0:unit, :]
    own_ref[...] = own.T[0:height, :]
    far = keep_ref[unit:, :] + got_ref[unit:, :]
    far_ref[...] = far.T[0:height, :]


def finish_body(own_ref, far_ref, out_ref):
    width = out_ref.shape[0]
    both = own_ref[...] + far_ref[...]
    out_ref[...] = both[0:width, :] / both[width : width + 1, :]


def small_call(body, shapes, name, *args):
    return pl.pallas_call(
        body,
        out_shape=shapes,
        in_specs=[VMEM_SPEC] * len(args),
        out_specs=jax.tree.map(lambda _: VMEM_SPEC, shapes),
        compiler_params=pltpu.CompilerParams(vmem_limit_bytes=8 * MIB),
        name=name,
    )(*args)


def grid_device(points, vectors):
    n_col = lax.axis_size("col")
    unit = points.shape[0]
    width = vectors.shape[1]
    points_all = float(unit * n_col * lax.axis_size("row"))
    n_units = n_col // 2

    def across(x, mask):
        return lax.ppermute(x, "col", [(i, i ^ mask) for i in range(n_col)])

    def sibling(x):
        return lax.ppermute(x, "row", [(0, 1), (1, 0)])

    def units(x):
        held = {0: x}
        bit = n_units // 2
        while bit:
            for u in list(held):
                held[u | bit] = across(held[u], bit)
            bit //= 2
        return [held[u] for u in range(n_units)]

    far = across(points, n_units)
    cols = units(points)
    rows = [points, sibling(points), far, sibling(far)]
    vecs = units(vectors.T)
    k, sums = kernel_tile(rows, cols, (0, 0))
    all_sums = [sums] + [across(sums, u) for u in range(1, n_units)]
    keep, give, log_density = product_tile(k, all_sums, vecs, points_all)
    got = sibling(give)
    shape = jax.ShapeDtypeStruct((width + 8, unit), jnp.float32)
    own, away = small_call(halves_body, (shape, shape), "halves", keep, got)
    back = across(away, n_units)
    smoothed = small_call(
        finish_body, jax.ShapeDtypeStruct((width, unit), jnp.float32), "finish", own, back
    )
    return (smoothed.T, log_density.reshape(unit))


def solution(mesh):
    n_col = mesh.shape["col"]
    n_row = mesh.shape["row"]
    placed = (P(("parts", "row", "col"), None), P(("parts", "row", "col"), None))

    def run(points, vectors):
        unit, feats = points.shape
        paired = n_row == 2 and n_col >= 2 and n_col & (n_col - 1) == 0
        tile_bytes = 4 * (4 * unit) * (n_col // 2 * unit)
        shaped = unit % 512 == 0 and feats == 128 and vectors.shape[1] <= 120
        if paired and shaped and tile_bytes <= 16 * MIB:
            return grid_device(points, vectors)
        return plain_device(points, vectors)

    return jax.shard_map(
        run,
        mesh=mesh,
        in_specs=placed,
        out_specs=(P(("parts", "row", "col"), None), P(("parts", "row", "col"))),
        check_vma=False,
    )
```

```python
import functools
import math

import jax
import jax.numpy as jnp
from jax import lax
from jax.experimental import pallas as pl
from jax.experimental.pallas import tpu as pltpu
from jax.sharding import PartitionSpec as P

MIB = 2**20
NT = (((1,), (1,)), ((), ()))
VMEM_SPEC = pl.BlockSpec(memory_space=pltpu.VMEM)


def by_blocks(piece, tile_fn):
    count = piece.shape[0]
    size = 512
    groups = piece.reshape(count // size, size, piece.shape[1])
    firsts = jnp.arange(count // size, dtype=jnp.int32) * size
    return lax.map(lambda item: tile_fn(item[0], item[1]), (groups, firsts))


def plain_device(points, vectors):
    rows_dev = points.shape[0]
    feats = points.shape[1]
    n_col = lax.axis_size("col")
    n_row = lax.axis_size("row")
    half = rows_dev * n_col
    total_pts = half * n_row
    row_pos = lax.axis_index("row")
    col_pos = lax.axis_index("col")
    width = 1.05 * math.sqrt(feats)
    col_points = lax.all_gather(points, "row", axis=0, tiled=True)
    col_vectors = lax.all_gather(vectors, "row", axis=0, tiled=True)
    local = jnp.arange(n_row * rows_dev, dtype=jnp.int32)
    col_ids = local // rows_dev * half + col_pos * rows_dev + local % rows_dev
    col_norms = jnp.sum(col_points.astype(jnp.float32) ** 2, axis=1)
    row_base = row_pos * half
    piece = lax.all_gather(points, "col", axis=0, tiled=True)

    def kernel_tile(block, first):
        norms = jnp.sum(block.astype(jnp.float32) ** 2, axis=1)
        cross = lax.dot_general(block, col_points, NT, preferred_element_type=jnp.float32)
        dist = norms[:, None] + col_norms[None, :] - 2.0 * cross
        values = jnp.exp((2.0 * feats - dist) / width)
        rows = row_base + first + jnp.arange(block.shape[0], dtype=jnp.int32)
        return jnp.where(rows[:, None] == col_ids[None, :], jnp.zeros_like(values), values)

    sums = by_blocks(piece, lambda block, first: jnp.sum(kernel_tile(block, first), axis=1))
    own_sums = lax.psum_scatter(sums.reshape(-1), "col", scatter_dimension=0, tiled=True)
    own_density = own_sums / total_pts
    col_density = lax.all_gather(own_density, "row", axis=0, tiled=True)

    def product_tile(block, first):
        weight = kernel_tile(block, first) / col_density[None, :]
        degree = jnp.sum(weight, axis=1)
        numer = jnp.dot(
            weight.astype(jnp.bfloat16), col_vectors, preferred_element_type=jnp.float32
        )
        return (numer, degree)

    numer, degree = by_blocks(piece, product_tile)
    numer = numer.reshape(piece.shape[0], vectors.shape[1])
    numer_own = lax.psum_scatter(numer, "col", scatter_dimension=0, tiled=True)
    degree_own = lax.psum_scatter(
        degree.reshape(-1), "col", scatter_dimension=0, tiled=True
    )
    return (numer_own / degree_own[:, None], jnp.log(own_density))


def augment(pts, first):
    count, feats = pts.shape
    square = pts.astype(jnp.float32)
    square = square * square
    high = square.astype(jnp.bfloat16)
    low = (square - high.astype(jnp.float32)).astype(jnp.bfloat16)
    pair = jnp.concatenate([high, low], axis=1)
    norm = jnp.dot(
        pair, jnp.ones((2 * feats, 128), jnp.bfloat16), preferred_element_type=jnp.float32
    )
    q = 0.5 * feats - 0.5 * norm
    q0 = q.astype(jnp.bfloat16).astype(jnp.float32)
    rest = q - q0
    q1 = rest.astype(jnp.bfloat16).astype(jnp.float32)
    q2 = rest - q1
    lane = lax.broadcasted_iota(jnp.int32, (count, 128), 1)
    other = 3 - first
    extra = jnp.where((lane >= other) & (lane < other + 3), 1.0, 0.0)
    extra = jnp.where(lane == first + 2, q2, extra)
    extra = jnp.where(lane == first + 1, q1, extra)
    extra = jnp.where(lane == first, q0, extra)
    return jnp.concatenate([pts, extra.astype(jnp.bfloat16)], axis=1)


def kernel_body(counts, unit, scale, diagonal, bm, bn, *refs):
    refs = list(refs)
    raw_rows, done_rows, raw_cols, done_cols, before = [
        [refs.pop(0) for _ in range(count)] for count in counts
    ]
    k_ref, sum_ref = refs.pop(0), refs.pop(0)
    if raw_rows:
        made = refs.pop(0)
        for u, ref in enumerate(raw_rows):
            made[u * unit : (u + 1) * unit, :] = augment(ref[...], 0)
        done_rows = [made] + done_rows
    if raw_cols:
        made = refs.pop(0)
        for u, ref in enumerate(raw_cols):
            made[u * unit : (u + 1) * unit, :] = augment(ref[...], 3)
        done_cols = done_cols + [made]
    c_at = 0
    for col_ref in done_cols:
        for c0 in range(0, col_ref.shape[0], bn):
            total = jnp.zeros((8, bn), jnp.float32)
            r_at = 0
            for row_ref in done_rows:
                for r0 in range(0, row_ref.shape[0], bm):
                    half_log = lax.dot_general(
                        row_ref[r0 : r0 + bm, :],
                        col_ref[c0 : c0 + bn, :],
                        NT,
                        preferred_element_type=jnp.float32,
                    )
                    value = jnp.exp2(half_log * scale)
                    if diagonal and r_at // unit == 0 and c_at // unit == 0:
                        i = lax.broadcasted_iota(jnp.int32, (bm, bn), 0) + r_at
                        j = lax.broadcasted_iota(jnp.int32, (bm, bn), 1) + c_at
                        value = jnp.where(i == j, 0.0, value)
                    k_ref[r_at : r_at + bm, c_at : c_at + bn] = value
                    total = total + jnp.sum(value.reshape(bm // 8, 8, bn), axis=0)
                    r_at += bm
            out = jnp.sum(total, axis=0, keepdims=True)
            at = 0
            for ref in before:
                if at <= c_at < at + ref.shape[1]:
                    out = out + ref[:, c_at - at : c_at - at + bn]
                at += ref.shape[1]
            sum_ref[0:1, c_at : c_at + bn] = out
            c_at += bn


def on_chip(body, shapes, name, limit, flops, *args):
    moved = sum(math.prod(x.shape) * x.dtype.itemsize for x in args)
    return pl.pallas_call(
        body,
        out_shape=shapes,
        in_specs=[VMEM_SPEC] * len(args),
        out_specs=tuple(VMEM_SPEC for _ in shapes),
        compiler_params=pltpu.CompilerParams(vmem_limit_bytes=limit * MIB),
        cost_estimate=pl.CostEstimate(
            flops=int(flops), bytes_accessed=moved, transcendentals=0
        ),
        name=name,
    )(*args)


def kernel_tile(raw_rows, done_rows, raw_cols, done_cols, before, diagonal, name):
    groups = [raw_rows, done_rows, raw_cols, done_cols, before]
    unit, feats = (raw_rows + raw_cols)[0].shape
    wide = feats + 128
    n_rows = sum(x.shape[0] for x in raw_rows + done_rows)
    n_cols = sum(x.shape[0] for x in raw_cols + done_cols)
    scale = 2.0 * math.log2(math.e) / (1.05 * math.sqrt(feats))
    shapes = [
        pltpu.VMEM((n_rows, n_cols), jnp.float32),
        pltpu.VMEM((1, n_cols), jnp.float32),
    ]
    for raw in (raw_rows, raw_cols):
        if raw:
            shapes.append(pltpu.VMEM((len(raw) * unit, wide), jnp.bfloat16))
    body = functools.partial(
        kernel_body, [len(g) for g in groups], unit, scale, diagonal, 256, 512
    )
    args = [x for g in groups for x in g]
    return on_chip(body, tuple(shapes), name, 12, 4 * n_rows * n_cols * wide, *args)


def density_body(n_cols, unit, points_all, *refs):
    sums = refs[:n_cols]
    vecs = refs[n_cols : 2 * n_cols]
    inverse_ref, vec_all, log_ref = refs[2 * n_cols :]
    width = vecs[0].shape[0]
    for v in range(n_cols):
        total = sums[0][:, v * unit : (v + 1) * unit]
        for u in range(1, n_cols):
            w = v ^ u
            total = total + sums[u][:, w * unit : (w + 1) * unit]
        density = total / points_all
        if v == 0:
            log_ref[...] = jnp.log(density)
        inverse_ref[:, v * unit : (v + 1) * unit] = 1.0 / density
        vec_all[0:width, v * unit : (v + 1) * unit] = vecs[v][...]
    ones = lax.broadcasted_iota(jnp.int32, (128 - width, n_cols * unit), 0) == 0
    vec_all[width:128, :] = jnp.where(ones, 1.0, 0.0).astype(jnp.bfloat16)


def product(out_ref, k_refs, r0, count, inverse_ref, vec_all, bm):
    for r in range(0, count, bm):
        numer = None
        at = 0
        for k_ref in k_refs:
            cols = slice(at, at + k_ref.shape[1])
            weight = k_ref[r0 + r : r0 + r + bm, :] * inverse_ref[:, cols]
            part = lax.dot_general(
                weight.astype(jnp.bfloat16),
                vec_all[:, cols],
                NT,
                preferred_element_type=jnp.float32,
            )
            numer = part if numer is None else numer + part
            at += k_ref.shape[1]
        out_ref[r : r + bm, :] = numer


def first_product_body(n_cols, unit, points_all, bm, k_ref, *refs):
    out_ref, *made = refs[2 * n_cols :]
    density_body(n_cols, unit, points_all, *refs[: 2 * n_cols], *made)
    product(out_ref, [k_ref], 0, k_ref.shape[0], made[0], made[1], bm)


def next_product_body(n_k, r0, bm, *refs):
    inverse_ref, vec_all, out_ref = refs[n_k:]
    product(out_ref, refs[:n_k], r0, out_ref.shape[0], inverse_ref, vec_all, bm)


def far_body(width, keep_ref, got_ref, out_ref):
    both = (keep_ref[...] + got_ref[...]).T
    high = both[width : width + 1, :].astype(jnp.bfloat16).astype(jnp.float32)
    low = both[width : width + 1, :] - high
    zero = jnp.zeros((14, both.shape[1]), jnp.float32)
    out = jnp.concatenate([both[0:width, :], high, low, zero], axis=0)
    out_ref[...] = out.astype(jnp.bfloat16)


def finish_body(own_ref, got_ref, far_ref, out_ref):
    width = out_ref.shape[0]
    near = (own_ref[...] + got_ref[...]).T
    far = far_ref[...].astype(jnp.float32)
    degree = near[width : width + 1, :] + (
        far[width : width + 1, :] + far[width + 1 : width + 2, :]
    )
    out_ref[...] = (near[0:width, :] + far[0:width, :]) / degree


def grid_device(points, vectors):
    n_col = lax.axis_size("col")
    unit = points.shape[0]
    width = vectors.shape[1]
    points_all = float(unit * n_col * lax.axis_size("row"))
    n_units = n_col // 2
    n_wide = n_units * unit

    def across(x, mask):
        return lax.ppermute(x, "col", [(i, i ^ mask) for i in range(n_col)])

    def sibling(x):
        return lax.ppermute(x, "row", [(0, 1), (1, 0)])

    beside = sibling(points)
    far = across(points, n_units)
    held = {0: points}
    bit = n_units // 2
    while bit:
        for u in list(held):
            held[u | bit] = across(held[u], bit)
        bit //= 2
    cols = [held[u] for u in range(n_units)]
    far_beside = sibling(far)
    k_near, sums, rows_near, cols_near = kernel_tile(
        [points, beside], [], cols[:-1], [], [], True, "near"
    )
    k_last, sums_last, cols_last = kernel_tile(
        [], [rows_near], cols[-1:], [], [], False, "last"
    )
    cols_all = [cols_near, cols_last]
    k_far, sums, _ = kernel_tile([far], [], [], cols_all, [sums, sums_last], False, "far")
    k_beside, sums, _ = kernel_tile(
        [far_beside], [], [], cols_all, [sums], False, "far_beside"
    )
    vecs = [vectors.T] + [across(vectors.T, u) for u in range(1, n_units)]
    all_sums = [sums] + [across(sums, u) for u in range(1, n_units)]

    flops = 2 * unit * n_wide * 128
    block = pltpu.VMEM((unit, 128), jnp.float32)
    give_far, inverse, vec_all, log_density = on_chip(
        functools.partial(first_product_body, n_units, unit, points_all, 256),
        (
            block,
            pltpu.VMEM((1, n_wide), jnp.float32),
            pltpu.VMEM((128, n_wide), jnp.bfloat16),
            jax.ShapeDtypeStruct((1, unit), jnp.float32),
        ),
        "product_far_beside",
        8,
        flops,
        k_beside,
        *all_sums,
        *vecs,
    )

    def next_product(ks, r0, name):
        body = functools.partial(next_product_body, len(ks), r0, 256)
        return on_chip(body, (block,), name, 8, flops, *ks, inverse, vec_all)[0]

    got_far = sibling(give_far)
    keep_far = next_product([k_far], 0, "product_far")
    (away,) = on_chip(
        functools.partial(far_body, width),
        (pltpu.VMEM((width + 16, unit), jnp.bfloat16),),
        "sum_far",
        8,
        1,
        keep_far,
        got_far,
    )
    back = across(away, n_units)
    give = next_product([k_near, k_last], unit, "product_beside")
    got = sibling(give)
    keep = next_product([k_near, k_last], 0, "product_own")
    (smoothed,) = on_chip(
        finish_body,
        (jax.ShapeDtypeStruct((width, unit), jnp.float32),),
        "finish",
        8,
        1,
        keep,
        got,
        back,
    )
    return (smoothed.T, log_density.reshape(unit))


def solution(mesh):
    n_col = mesh.shape["col"]
    n_row = mesh.shape["row"]
    placed = (P(("parts", "row", "col"), None), P(("parts", "row", "col"), None))

    def run(points, vectors):
        unit, feats = points.shape
        paired = n_row == 2 and n_col >= 2 and n_col & (n_col - 1) == 0
        tile_bytes = 4 * (4 * unit) * (n_col // 2 * unit)
        shaped = unit % 512 == 0 and feats == 128 and vectors.shape[1] <= 120
        if paired and shaped and tile_bytes <= 16 * MIB:
            return grid_device(points, vectors)
        return plain_device(points, vectors)

    return jax.shard_map(
        run,
        mesh=mesh,
        in_specs=placed,
        out_specs=(P(("parts", "row", "col"), None), P(("parts", "row", "col"))),
        check_vma=False,
    )
```

```python
import functools
import math

import jax
import jax.numpy as jnp
from jax import lax
from jax.experimental import pallas as pl
from jax.experimental.pallas import tpu as pltpu
from jax.sharding import PartitionSpec as P

MIB = 2**20
NT = (((1,), (1,)), ((), ()))
VMEM_SPEC = pl.BlockSpec(memory_space=pltpu.VMEM)


def by_blocks(piece, tile_fn):
    count = piece.shape[0]
    size = 512
    groups = piece.reshape(count // size, size, piece.shape[1])
    firsts = jnp.arange(count // size, dtype=jnp.int32) * size
    return lax.map(lambda item: tile_fn(item[0], item[1]), (groups, firsts))


def plain_device(points, vectors):
    rows_dev = points.shape[0]
    feats = points.shape[1]
    n_col = lax.axis_size("col")
    n_row = lax.axis_size("row")
    half = rows_dev * n_col
    total_pts = half * n_row
    row_pos = lax.axis_index("row")
    col_pos = lax.axis_index("col")
    width = 1.05 * math.sqrt(feats)
    col_points = lax.all_gather(points, "row", axis=0, tiled=True)
    col_vectors = lax.all_gather(vectors, "row", axis=0, tiled=True)
    local = jnp.arange(n_row * rows_dev, dtype=jnp.int32)
    col_ids = local // rows_dev * half + col_pos * rows_dev + local % rows_dev
    col_norms = jnp.sum(col_points.astype(jnp.float32) ** 2, axis=1)
    row_base = row_pos * half
    piece = lax.all_gather(points, "col", axis=0, tiled=True)

    def kernel_tile(block, first):
        norms = jnp.sum(block.astype(jnp.float32) ** 2, axis=1)
        cross = lax.dot_general(block, col_points, NT, preferred_element_type=jnp.float32)
        dist = norms[:, None] + col_norms[None, :] - 2.0 * cross
        values = jnp.exp((2.0 * feats - dist) / width)
        rows = row_base + first + jnp.arange(block.shape[0], dtype=jnp.int32)
        return jnp.where(rows[:, None] == col_ids[None, :], jnp.zeros_like(values), values)

    sums = by_blocks(piece, lambda block, first: jnp.sum(kernel_tile(block, first), axis=1))
    own_sums = lax.psum_scatter(sums.reshape(-1), "col", scatter_dimension=0, tiled=True)
    own_density = own_sums / total_pts
    col_density = lax.all_gather(own_density, "row", axis=0, tiled=True)

    def product_tile(block, first):
        weight = kernel_tile(block, first) / col_density[None, :]
        degree = jnp.sum(weight, axis=1)
        numer = jnp.dot(
            weight.astype(jnp.bfloat16), col_vectors, preferred_element_type=jnp.float32
        )
        return (numer, degree)

    numer, degree = by_blocks(piece, product_tile)
    numer = numer.reshape(piece.shape[0], vectors.shape[1])
    numer_own = lax.psum_scatter(numer, "col", scatter_dimension=0, tiled=True)
    degree_own = lax.psum_scatter(
        degree.reshape(-1), "col", scatter_dimension=0, tiled=True
    )
    return (numer_own / degree_own[:, None], jnp.log(own_density))


def augment(pts, first):
    count, feats = pts.shape
    square = pts.astype(jnp.float32)
    square = square * square
    high = square.astype(jnp.bfloat16)
    low = (square - high.astype(jnp.float32)).astype(jnp.bfloat16)
    pair = jnp.concatenate([high, low], axis=1)
    norm = jnp.dot(
        pair, jnp.ones((2 * feats, 128), jnp.bfloat16), preferred_element_type=jnp.float32
    )
    q = 0.5 * feats - 0.5 * norm
    q0 = q.astype(jnp.bfloat16).astype(jnp.float32)
    rest = q - q0
    q1 = rest.astype(jnp.bfloat16).astype(jnp.float32)
    q2 = rest - q1
    lane = lax.broadcasted_iota(jnp.int32, (count, 128), 1)
    other = 3 - first
    extra = jnp.where((lane >= other) & (lane < other + 3), 1.0, 0.0)
    extra = jnp.where(lane == first + 2, q2, extra)
    extra = jnp.where(lane == first + 1, q1, extra)
    extra = jnp.where(lane == first, q0, extra)
    return jnp.concatenate([pts, extra.astype(jnp.bfloat16)], axis=1)


def kernel_body(counts, unit, scale, diagonal, bm, bn, *refs):
    refs = list(refs)
    raw_rows, done_rows, raw_cols, done_cols, before, vectors = [
        [refs.pop(0) for _ in range(count)] for count in counts
    ]
    k_ref, sum_ref = refs.pop(0), refs.pop(0)
    pack_ref = refs.pop(0) if vectors else None
    if raw_cols:
        made = refs.pop(0)
        for u, ref in enumerate(raw_cols):
            made[u * unit : (u + 1) * unit, :] = augment(ref[...], 3)
        done_cols = done_cols + [made]
    if raw_rows:
        made = refs.pop(0)
        for u, ref in enumerate(raw_rows):
            made[u * unit : (u + 1) * unit, :] = augment(ref[...], 0)
        done_rows = done_rows + [made]
    c_at = 0
    for col_ref in done_cols:
        for c0 in range(0, col_ref.shape[0], bn):
            total = jnp.zeros((8, bn), jnp.float32)
            r_at = 0
            for row_ref in done_rows:
                for r0 in range(0, row_ref.shape[0], bm):
                    half_log = lax.dot_general(
                        row_ref[r0 : r0 + bm, :],
                        col_ref[c0 : c0 + bn, :],
                        NT,
                        preferred_element_type=jnp.float32,
                    )
                    value = jnp.exp2(half_log * scale)
                    if diagonal and r_at // unit == 0 and c_at // unit == 0:
                        i = lax.broadcasted_iota(jnp.int32, (bm, bn), 0) + r_at
                        j = lax.broadcasted_iota(jnp.int32, (bm, bn), 1) + c_at
                        value = jnp.where(i == j, 0.0, value)
                    k_ref[r_at : r_at + bm, c_at : c_at + bn] = value
                    total = total + jnp.sum(value.reshape(bm // 8, 8, bn), axis=0)
                    r_at += bm
            out = jnp.sum(total, axis=0, keepdims=True)
            at = 0
            for ref in before:
                if at <= c_at < at + ref.shape[1]:
                    out = out + ref[:, c_at - at : c_at - at + bn]
                at += ref.shape[1]
            sum_ref[0:1, c_at : c_at + bn] = out
            c_at += bn
    for ref in vectors:
        width = ref.shape[0]
        terms = []
        for at in range(0, c_at, unit):
            terms.extend(three_terms(sum_ref[0:1, at : at + unit]))
        terms.append(jnp.zeros((16 - len(terms), unit), jnp.float32))
        pack_ref[0:width, :] = ref[...]
        pack_ref[width:, :] = jnp.concatenate(terms, axis=0).astype(jnp.bfloat16)


def on_chip(body, shapes, name, limit, *args, scratch=()):
    return pl.pallas_call(
        body,
        out_shape=tuple(shapes),
        in_specs=[VMEM_SPEC] * len(args),
        out_specs=tuple(VMEM_SPEC for _ in shapes),
        scratch_shapes=list(scratch),
        compiler_params=pltpu.CompilerParams(vmem_limit_bytes=limit * MIB),
        name=name,
    )(*args)


def kernel_tile(name, raw_rows, done_rows, raw_cols, done_cols, before=(), vectors=(), **kw):
    diagonal = kw.get("diagonal", False)
    groups = [raw_rows, done_rows, raw_cols, done_cols, before, vectors]
    unit, feats = (raw_rows + raw_cols)[0].shape
    wide = feats + 128
    n_rows = unit * len(raw_rows) + sum(x.shape[0] for x in done_rows)
    n_cols = unit * len(raw_cols) + sum(x.shape[0] for x in done_cols)
    scale = 2.0 * math.log2(math.e) / (1.05 * math.sqrt(feats))
    shapes = [
        pltpu.VMEM((n_rows, n_cols), jnp.float32),
        pltpu.VMEM((1, n_cols), jnp.float32),
    ]
    for x in vectors:
        shapes.append(pltpu.VMEM((x.shape[0] + 16, unit), jnp.bfloat16))
    scratch = []
    if raw_cols:
        shapes.append(pltpu.VMEM((len(raw_cols) * unit, wide), jnp.bfloat16))
    if raw_rows:
        made = pltpu.VMEM((len(raw_rows) * unit, wide), jnp.bfloat16)
        (shapes if raw_cols else scratch).append(made)
    counts = [len(g) for g in groups]
    body = functools.partial(kernel_body, counts, unit, scale, diagonal, 256, 512)
    args = [x for g in groups for x in g]
    return on_chip(body, shapes, name, 12, *args, scratch=scratch)


def own_body(points_ref, vector_ref, row_ref, col_ref, copy_ref):
    row_ref[...] = augment(points_ref[...], 0)
    col_ref[...] = augment(points_ref[...], 3)
    copy_ref[...] = vector_ref[...]


def three_terms(x):
    high = x.astype(jnp.bfloat16).astype(jnp.float32)
    rest = x - high
    middle = rest.astype(jnp.bfloat16).astype(jnp.float32)
    return high, middle, rest - middle


def density_body(unit, points_all, own_ref, packs, vec_all, inverse_ref, density_ref):
    n_cols = len(packs)
    width = packs[0].shape[0] - 16
    given = [None] + [ref[width:, :].astype(jnp.float32) for ref in packs[1:]]
    for v in range(n_cols):
        cols = slice(v * unit, (v + 1) * unit)
        total = own_ref[:, cols]
        for u in range(1, n_cols):
            w = 3 * (v ^ u)
            row = given[u]
            total = total + (row[w : w + 1] + (row[w + 1 : w + 2] + row[w + 2 : w + 3]))
        density = total / points_all
        if v == 0:
            density_ref[...] = density
        inverse_ref[:, cols] = 1.0 / density
        vec_all[0:width, cols] = packs[v][0:width, :]
    ones = lax.broadcasted_iota(jnp.int32, (128 - width, n_cols * unit), 0) == 0
    vec_all[width:128, :] = jnp.where(ones, 1.0, 0.0).astype(jnp.bfloat16)


def product(out_ref, k_refs, r0, count, inverse_ref, vec_all, bm):
    for r in range(0, count, bm):
        numer = None
        at = 0
        for k_ref in k_refs:
            cols = slice(at, at + k_ref.shape[1])
            weight = k_ref[r0 + r : r0 + r + bm, :] * inverse_ref[:, cols]
            part = lax.dot_general(
                weight.astype(jnp.bfloat16),
                vec_all[:, cols],
                NT,
                preferred_element_type=jnp.float32,
            )
            numer = part if numer is None else numer + part
            at += k_ref.shape[1]
        out_ref[r : r + bm, :] = numer


def first_product_body(unit, points_all, bm, k_ref, own_ref, *refs):
    *packs, out_ref, vec_all, inverse_ref, density_ref = refs
    density_body(unit, points_all, own_ref, packs, vec_all, inverse_ref, density_ref)
    product(out_ref, [k_ref], 0, k_ref.shape[0], inverse_ref, vec_all, bm)


def next_product_body(n_k, r0, bm, *refs):
    inverse_ref, vec_all, out_ref = refs[n_k:]
    product(out_ref, refs[:n_k], r0, out_ref.shape[0], inverse_ref, vec_all, bm)


def far_body(width, keep_ref, got_ref, out_ref):
    both = (keep_ref[...] + got_ref[...]).T
    high = both[width : width + 1, :].astype(jnp.bfloat16).astype(jnp.float32)
    low = both[width : width + 1, :] - high
    zero = jnp.zeros((14, both.shape[1]), jnp.float32)
    out = jnp.concatenate([both[0:width, :], high, low, zero], axis=0)
    out_ref[...] = out.astype(jnp.bfloat16)


def near_body(own_ref, got_ref, density_ref, out_ref, log_ref):
    log_ref[...] = jnp.log(density_ref[...])
    out_ref[...] = (own_ref[...] + got_ref[...]).T[0 : out_ref.shape[0], :]


def finish_body(near_ref, far_ref, out_ref):
    width = out_ref.shape[0]
    far = far_ref[...].astype(jnp.float32)
    degree = near_ref[width : width + 1, :] + (
        far[width : width + 1, :] + far[width + 1 : width + 2, :]
    )
    out_ref[...] = (near_ref[0:width, :] + far[0:width, :]) / degree


def after(x, *others):
    return lax.optimization_barrier((x, *others))[0]


def grid_device(points, vectors):
    n_col = lax.axis_size("col")
    unit, feats = points.shape
    width = vectors.shape[1]
    points_all = float(unit * n_col * lax.axis_size("row"))
    n_units = n_col // 2
    n_wide = n_units * unit

    def across(x, mask):
        return lax.ppermute(x, "col", [(i, i ^ mask) for i in range(n_col)])

    def sibling(x):
        return lax.ppermute(x, "row", [(0, 1), (1, 0)])

    far = across(points, n_units)
    beside = sibling(points)
    augmented = pltpu.VMEM((unit, feats + 128), jnp.bfloat16)
    row_own, col_own, vec_own = on_chip(
        own_body,
        (augmented, augmented, pltpu.VMEM((width, unit), jnp.bfloat16)),
        "own",
        8,
        points,
        vectors.T,
    )
    held = {0: points}
    bit = n_units // 2
    while bit:
        for u in list(held):
            held[u | bit] = across(after(held[u], col_own) if u else held[u], bit)
        bit //= 2
    cols = [held[u] for u in range(1, n_units)]
    k_near, sums_near, cols_near, row_beside = kernel_tile(
        "near", [beside], [row_own], cols[:-1], [col_own], diagonal=True
    )
    far_beside = sibling(after(far, sums_near))
    k_last, sums_last, cols_last = kernel_tile(
        "last", [], [row_own, row_beside], cols[-1:], []
    )
    cols_all = [col_own, cols_near, cols_last]
    k_far, sums = kernel_tile("far", [far], [], [], cols_all, [sums_near, sums_last])
    k_beside, sums, pack = kernel_tile(
        "far_beside", [far_beside], [], [], cols_all, [sums], [vec_own]
    )
    packs = [pack] + [across(pack, u) for u in range(1, n_units)]

    block = pltpu.VMEM((unit, 128), jnp.float32)
    give_far, vec_all, inverse, density = on_chip(
        functools.partial(first_product_body, unit, points_all, 256),
        (
            block,
            pltpu.VMEM((128, n_wide), jnp.bfloat16),
            pltpu.VMEM((1, n_wide), jnp.float32),
            pltpu.VMEM((1, unit), jnp.float32),
        ),
        "product_far_beside",
        8,
        k_beside,
        sums,
        *packs,
    )

    def next_product(name, ks, r0):
        body = functools.partial(next_product_body, len(ks), r0, 256)
        return on_chip(body, (block,), name, 8, *ks, inverse, vec_all)[0]

    got_far = sibling(give_far)
    keep_far = next_product("product_far", [k_far], 0)
    (away,) = on_chip(
        functools.partial(far_body, width),
        (pltpu.VMEM((width + 16, unit), jnp.bfloat16),),
        "sum_far",
        8,
        keep_far,
        got_far,
    )
    back = across(away, n_units)
    got = sibling(next_product("product_beside", [k_near, k_last], unit))
    keep = next_product("product_own", [k_near, k_last], 0)
    near, log_density = on_chip(
        near_body,
        (
            pltpu.VMEM((width + 8, unit), jnp.float32),
            jax.ShapeDtypeStruct((1, unit), jnp.float32),
        ),
        "sum_near",
        8,
        keep,
        got,
        density,
    )
    (smoothed,) = on_chip(
        finish_body,
        (jax.ShapeDtypeStruct((width, unit), jnp.float32),),
        "finish",
        8,
        near,
        back,
    )
    return (smoothed.T, log_density.reshape(unit))


def solution(mesh):
    n_col = mesh.shape["col"]
    n_row = mesh.shape["row"]
    placed = (P(("parts", "row", "col"), None), P(("parts", "row", "col"), None))

    def run(points, vectors):
        unit, feats = points.shape
        paired = n_row == 2 and n_col >= 8 and n_col & (n_col - 1) == 0
        tile_bytes = 4 * (4 * unit) * (n_col // 2 * unit)
        width = vectors.shape[1]
        shaped = unit % 512 == 0 and feats == 128 and width % 16 == 0 and width <= 112
        few = 3 * (n_col // 2) <= 16
        if paired and shaped and few and tile_bytes <= 16 * MIB:
            return grid_device(points, vectors)
        return plain_device(points, vectors)

    return jax.shard_map(
        run,
        mesh=mesh,
        in_specs=placed,
        out_specs=(P(("parts", "row", "col"), None), P(("parts", "row", "col"))),
        check_vma=False,
    )
```

```python
import functools
import math

import jax
import jax.numpy as jnp
from jax import lax
from jax.experimental import pallas as pl
from jax.experimental.pallas import tpu as pltpu
from jax.sharding import PartitionSpec as P

MIB = 2**20
NT = (((1,), (1,)), ((), ()))
VMEM_SPEC = pl.BlockSpec(memory_space=pltpu.VMEM)


def by_blocks(piece, tile_fn):
    count = piece.shape[0]
    size = 512
    groups = piece.reshape(count // size, size, piece.shape[1])
    firsts = jnp.arange(count // size, dtype=jnp.int32) * size
    return lax.map(lambda item: tile_fn(item[0], item[1]), (groups, firsts))


def plain_device(points, vectors):
    rows_dev = points.shape[0]
    feats = points.shape[1]
    n_col = lax.axis_size("col")
    n_row = lax.axis_size("row")
    half = rows_dev * n_col
    total_pts = half * n_row
    row_pos = lax.axis_index("row")
    col_pos = lax.axis_index("col")
    width = 1.05 * math.sqrt(feats)
    col_points = lax.all_gather(points, "row", axis=0, tiled=True)
    col_vectors = lax.all_gather(vectors, "row", axis=0, tiled=True)
    local = jnp.arange(n_row * rows_dev, dtype=jnp.int32)
    col_ids = local // rows_dev * half + col_pos * rows_dev + local % rows_dev
    col_norms = jnp.sum(col_points.astype(jnp.float32) ** 2, axis=1)
    row_base = row_pos * half
    piece = lax.all_gather(points, "col", axis=0, tiled=True)

    def kernel_tile(block, first):
        norms = jnp.sum(block.astype(jnp.float32) ** 2, axis=1)
        cross = lax.dot_general(block, col_points, NT, preferred_element_type=jnp.float32)
        dist = norms[:, None] + col_norms[None, :] - 2.0 * cross
        values = jnp.exp((2.0 * feats - dist) / width)
        rows = row_base + first + jnp.arange(block.shape[0], dtype=jnp.int32)
        return jnp.where(rows[:, None] == col_ids[None, :], jnp.zeros_like(values), values)

    sums = by_blocks(piece, lambda block, first: jnp.sum(kernel_tile(block, first), axis=1))
    own_sums = lax.psum_scatter(sums.reshape(-1), "col", scatter_dimension=0, tiled=True)
    own_density = own_sums / total_pts
    col_density = lax.all_gather(own_density, "row", axis=0, tiled=True)

    def product_tile(block, first):
        weight = kernel_tile(block, first) / col_density[None, :]
        degree = jnp.sum(weight, axis=1)
        numer = jnp.dot(
            weight.astype(jnp.bfloat16), col_vectors, preferred_element_type=jnp.float32
        )
        return (numer, degree)

    numer, degree = by_blocks(piece, product_tile)
    numer = numer.reshape(piece.shape[0], vectors.shape[1])
    numer_own = lax.psum_scatter(numer, "col", scatter_dimension=0, tiled=True)
    degree_own = lax.psum_scatter(
        degree.reshape(-1), "col", scatter_dimension=0, tiled=True
    )
    return (numer_own / degree_own[:, None], jnp.log(own_density))


def augment(pts, first):
    count, feats = pts.shape
    square = pts.astype(jnp.float32)
    square = square * square
    high = square.astype(jnp.bfloat16)
    low = (square - high.astype(jnp.float32)).astype(jnp.bfloat16)
    pair = jnp.concatenate([high, low], axis=1)
    norm = jnp.dot(
        pair, jnp.ones((2 * feats, 128), jnp.bfloat16), preferred_element_type=jnp.float32
    )
    q = 0.5 * feats - 0.5 * norm
    q0 = q.astype(jnp.bfloat16).astype(jnp.float32)
    rest = q - q0
    q1 = rest.astype(jnp.bfloat16).astype(jnp.float32)
    q2 = rest - q1
    lane = lax.broadcasted_iota(jnp.int32, (count, 128), 1)
    other = 3 - first
    extra = jnp.where((lane >= other) & (lane < other + 3), 1.0, 0.0)
    extra = jnp.where(lane == first + 2, q2, extra)
    extra = jnp.where(lane == first + 1, q1, extra)
    extra = jnp.where(lane == first, q0, extra)
    return jnp.concatenate([pts, extra.astype(jnp.bfloat16)], axis=1)


def kernel_body(counts, unit, scale, diagonal, bm, bn, *refs):
    refs = list(refs)
    raw_rows, done_rows, raw_cols, done_cols, before, ahead = [
        [refs.pop(0) for _ in range(count)] for count in counts
    ]
    k_ref, sum_ref = refs.pop(0), refs.pop(0)
    if raw_rows:
        made = refs.pop(0)
        for u, ref in enumerate(raw_rows):
            made[u * unit : (u + 1) * unit, :] = augment(ref[...], 0)
        done_rows = done_rows + [made]
    if raw_cols:
        made = refs.pop(0)
        for u, ref in enumerate(raw_cols):
            made[u * unit : (u + 1) * unit, :] = augment(ref[...], 3)
        done_cols = done_cols + [made]
    skip = 0
    for ref in ahead:
        sum_ref[0:1, skip : skip + ref.shape[1]] = ref[...]
        skip += ref.shape[1]
    c_at = 0
    for col_ref in done_cols:
        for c0 in range(0, col_ref.shape[0], bn):
            total = jnp.zeros((8, bn), jnp.float32)
            r_at = 0
            for row_ref in done_rows:
                for r0 in range(0, row_ref.shape[0], bm):
                    half_log = lax.dot_general(
                        row_ref[r0 : r0 + bm, :],
                        col_ref[c0 : c0 + bn, :],
                        NT,
                        preferred_element_type=jnp.float32,
                    )
                    value = jnp.exp2(half_log * scale)
                    if diagonal and r_at // unit == 0 and c_at // unit == 0:
                        i = lax.broadcasted_iota(jnp.int32, (bm, bn), 0) + r_at
                        j = lax.broadcasted_iota(jnp.int32, (bm, bn), 1) + c_at
                        value = jnp.where(i == j, 0.0, value)
                    k_ref[r_at : r_at + bm, c_at : c_at + bn] = value
                    total = total + jnp.sum(value.reshape(bm // 8, 8, bn), axis=0)
                    r_at += bm
            out = jnp.sum(total, axis=0, keepdims=True)
            at = 0
            for ref in before:
                if at <= c_at < at + ref.shape[1]:
                    out = out + ref[:, c_at - at : c_at - at + bn]
                at += ref.shape[1]
            sum_ref[0:1, skip + c_at : skip + c_at + bn] = out
            c_at += bn


def on_chip(body, shapes, name, limit, *args, scratch=()):
    return pl.pallas_call(
        body,
        out_shape=tuple(shapes),
        in_specs=[VMEM_SPEC] * len(args),
        out_specs=tuple(VMEM_SPEC for _ in shapes),
        scratch_shapes=list(scratch),
        compiler_params=pltpu.CompilerParams(vmem_limit_bytes=limit * MIB),
        name=name,
    )(*args)


def kernel_tile(
    name, raw_rows, done_rows, raw_cols, done_cols, before=(), ahead=(), diagonal=False
):
    groups = [raw_rows, done_rows, raw_cols, done_cols, before, ahead]
    unit, feats = (raw_rows + raw_cols)[0].shape
    wide = feats + 128
    n_rows = unit * len(raw_rows) + sum(x.shape[0] for x in done_rows)
    n_cols = unit * len(raw_cols) + sum(x.shape[0] for x in done_cols)
    scale = 2.0 * math.log2(math.e) / (1.05 * math.sqrt(feats))
    shapes = [
        pltpu.VMEM((n_rows, n_cols), jnp.float32),
        pltpu.VMEM((1, n_cols + sum(x.shape[1] for x in ahead)), jnp.float32),
    ]
    scratch = []
    for raw in (raw_rows, raw_cols):
        if raw:
            made = pltpu.VMEM((len(raw) * unit, wide), jnp.bfloat16)
            (scratch if ahead else shapes).append(made)
    counts = [len(g) for g in groups]
    body = functools.partial(kernel_body, counts, unit, scale, diagonal, 256, 512)
    args = [x for g in groups for x in g]
    return on_chip(body, shapes, name, 12, *args, scratch=scratch)


def own_body(points_ref, vector_ref, row_ref, col_ref, copy_ref):
    row_ref[...] = augment(points_ref[...], 0)
    col_ref[...] = augment(points_ref[...], 3)
    copy_ref[...] = vector_ref[...]


def vectors_body(*refs):
    *vecs, vec_all = refs
    width, unit = vecs[0].shape
    for v, ref in enumerate(vecs):
        vec_all[0:width, v * unit : (v + 1) * unit] = ref[...]
    ones = lax.broadcasted_iota(jnp.int32, (128 - width, len(vecs) * unit), 0) == 0
    vec_all[width:128, :] = jnp.where(ones, 1.0, 0.0).astype(jnp.bfloat16)


def density_body(unit, points_all, sums, inverse_ref, density_ref):
    n_cols = len(sums)
    for v in range(n_cols):
        cols = slice(v * unit, (v + 1) * unit)
        total = sums[0][:, cols]
        for u in range(1, n_cols):
            w = v ^ u
            total = total + sums[u][:, w * unit : (w + 1) * unit]
        density = total / points_all
        if v == 0:
            density_ref[...] = density
        inverse_ref[:, cols] = 1.0 / density


def product(k_refs, firsts, r, bm, inverse_ref, vec_all):
    numer = None
    at = 0
    for k_ref, first in zip(k_refs, firsts):
        cols = slice(at, at + k_ref.shape[1])
        weight = k_ref[first + r : first + r + bm, :] * inverse_ref[:, cols]
        part = lax.dot_general(
            weight.astype(jnp.bfloat16),
            vec_all[:, cols],
            NT,
            preferred_element_type=jnp.float32,
        )
        numer = part if numer is None else numer + part
        at += k_ref.shape[1]
    return numer.T


def give(out_ref, k_refs, firsts, inverse_ref, vec_all, bm):
    width = out_ref.shape[0] - 16
    for r in range(0, out_ref.shape[1], bm):
        numer = product(k_refs, firsts, r, bm, inverse_ref, vec_all)
        degree = numer[width : width + 1, :]
        high = degree.astype(jnp.bfloat16).astype(jnp.float32)
        zero = jnp.zeros((14, bm), jnp.float32)
        tail = jnp.concatenate([high, degree - high, zero], axis=0)
        out_ref[0:width, r : r + bm] = numer[0:width, :].astype(jnp.bfloat16)
        out_ref[width:, r : r + bm] = tail.astype(jnp.bfloat16)


def first_give_body(unit, points_all, first, bm, n_sums, k_near, k_side, vec_all, *refs):
    sums = refs[:n_sums]
    out_ref, inverse_ref, density_ref = refs[n_sums:]
    density_body(unit, points_all, sums, inverse_ref, density_ref)
    give(out_ref, [k_near, k_side], [first, first], inverse_ref, vec_all, bm)


def next_give_body(firsts, bm, *refs):
    *k_refs, vec_all, inverse_ref, out_ref = refs
    give(out_ref, k_refs, firsts, inverse_ref, vec_all, bm)


def keep_body(bm, *refs):
    *k_refs, vec_all, inverse_ref, density_ref, out_ref, log_ref = refs
    height, unit = out_ref.shape
    firsts = [0] * len(k_refs)
    for r in range(0, unit, bm):
        numer = product(k_refs, firsts, r, bm, inverse_ref, vec_all)
        out_ref[:, r : r + bm] = numer[0:height, :]
    log_ref[...] = jnp.log(density_ref[...])


def finish_body(near_ref, *refs):
    *far_refs, out_ref = refs
    width = out_ref.shape[0]
    numer = near_ref[0:width, :]
    degree = near_ref[width : width + 1, :]
    for ref in far_refs:
        far = ref[...].astype(jnp.float32)
        numer = numer + far[0:width, :]
        degree = degree + (far[width : width + 1, :] + far[width + 1 : width + 2, :])
    out_ref[...] = numer / degree


def after(x, *others):
    return lax.optimization_barrier((x, *others))[0]


def grid_device(points, vectors):
    n_col = lax.axis_size("col")
    unit, feats = points.shape
    width = vectors.shape[1]
    points_all = float(unit * n_col * lax.axis_size("row"))
    n_units = n_col // 2

    def across(x, mask):
        return lax.ppermute(x, "col", [(i, i ^ mask) for i in range(n_col)])

    def sibling(x):
        return lax.ppermute(x, "row", [(0, 1), (1, 0)])

    far = across(points, n_units)
    beside = sibling(points)
    augmented = pltpu.VMEM((unit, feats + 128), jnp.bfloat16)
    vec = vectors.T
    row_own, col_own, vec_own = on_chip(
        own_body,
        (augmented, augmented, pltpu.VMEM((width, unit), jnp.bfloat16)),
        "own",
        8,
        points,
        vec,
    )
    held = {0: points}
    bit = n_units // 2
    while bit:
        for u in list(held):
            held[u | bit] = across(held[u], bit)
        bit //= 2
    rows = [held[u] for u in range(1, n_units)]
    far_beside = sibling(after(far, col_own))
    n_wide = 4 * unit

    vec_far = across(after(vec, far), n_units)
    k_near, sums_near, rows_near, cols_near = kernel_tile(
        "near", rows[:-1], [row_own], [beside, far], [col_own], diagonal=True
    )
    k_last, sums_last, row_last = kernel_tile(
        "last", rows[-1:], [], [], [col_own, cols_near], [sums_near]
    )
    k_side, sums = kernel_tile(
        "side", [], [row_own, rows_near, row_last], [far_beside], [], [], [sums_last]
    )
    sums_far = across(sums, n_units)
    all_sums = [sums, sibling(sums), sums_far, sibling(sums_far)]

    vecs = [vec_own, sibling(vec), vec_far, sibling(after(vec_far, sums_far))]
    (vec_all,) = on_chip(
        vectors_body, (pltpu.VMEM((128, n_wide), jnp.bfloat16),), "vectors", 4, *vecs
    )

    packed = pltpu.VMEM((width + 16, unit), jnp.bfloat16)
    away, inverse, density = on_chip(
        functools.partial(first_give_body, unit, points_all, unit, 256, len(all_sums)),
        (
            packed,
            pltpu.VMEM((1, n_wide), jnp.float32),
            pltpu.VMEM((1, unit), jnp.float32),
        ),
        "give_first",
        8,
        k_near,
        k_side,
        vec_all,
        *all_sums,
    )
    back = [across(away, 1)]
    for u in range(2, n_units):
        last = u == n_units - 1
        (away,) = on_chip(
            functools.partial(next_give_body, [0 if last else u * unit, u * unit], 256),
            (packed,),
            "give",
            8,
            k_last if last else k_near,
            k_side,
            vec_all,
            after(inverse, away),
        )
        back.append(across(away, u))
    near, log_density = on_chip(
        functools.partial(keep_body, 256),
        (
            pltpu.VMEM((width + 8, unit), jnp.float32),
            jax.ShapeDtypeStruct((1, unit), jnp.float32),
        ),
        "keep",
        8,
        k_near,
        k_side,
        vec_all,
        inverse,
        density,
    )
    (smoothed,) = on_chip(
        finish_body,
        (jax.ShapeDtypeStruct((width, unit), jnp.float32),),
        "finish",
        8,
        near,
        *back,
    )
    return (smoothed.T, log_density.reshape(unit))


def solution(mesh):
    n_col = mesh.shape["col"]
    n_row = mesh.shape["row"]
    placed = (P(("parts", "row", "col"), None), P(("parts", "row", "col"), None))

    def run(points, vectors):
        unit, feats = points.shape
        paired = n_row == 2 and n_col >= 8 and n_col & (n_col - 1) == 0
        tile_bytes = 4 * (4 * unit) * (n_col // 2 * unit)
        width = vectors.shape[1]
        shaped = unit % 512 == 0 and feats == 128 and width % 16 == 0 and width <= 112
        if paired and shaped and tile_bytes <= 16 * MIB:
            return grid_device(points, vectors)
        return plain_device(points, vectors)

    return jax.shard_map(
        run,
        mesh=mesh,
        in_specs=placed,
        out_specs=(P(("parts", "row", "col"), None), P(("parts", "row", "col"))),
        check_vma=False,
    )
```

```python
import functools
import math

import jax
import jax.numpy as jnp
from jax import lax
from jax.experimental import pallas as pl
from jax.experimental.pallas import tpu as pltpu
from jax.sharding import PartitionSpec as P

MIB = 2**20
NT = (((1,), (1,)), ((), ()))
VMEM_SPEC = pl.BlockSpec(memory_space=pltpu.VMEM)


def by_blocks(piece, tile_fn):
    count = piece.shape[0]
    size = 512
    groups = piece.reshape(count // size, size, piece.shape[1])
    firsts = jnp.arange(count // size, dtype=jnp.int32) * size
    return lax.map(lambda item: tile_fn(item[0], item[1]), (groups, firsts))


def plain_device(points, vectors):
    rows_dev = points.shape[0]
    feats = points.shape[1]
    n_col = lax.axis_size("col")
    n_row = lax.axis_size("row")
    half = rows_dev * n_col
    total_pts = half * n_row
    row_pos = lax.axis_index("row")
    col_pos = lax.axis_index("col")
    width = 1.05 * math.sqrt(feats)
    col_points = lax.all_gather(points, "row", axis=0, tiled=True)
    col_vectors = lax.all_gather(vectors, "row", axis=0, tiled=True)
    local = jnp.arange(n_row * rows_dev, dtype=jnp.int32)
    col_ids = local // rows_dev * half + col_pos * rows_dev + local % rows_dev
    col_norms = jnp.sum(col_points.astype(jnp.float32) ** 2, axis=1)
    row_base = row_pos * half
    piece = lax.all_gather(points, "col", axis=0, tiled=True)

    def kernel_tile(block, first):
        norms = jnp.sum(block.astype(jnp.float32) ** 2, axis=1)
        cross = lax.dot_general(block, col_points, NT, preferred_element_type=jnp.float32)
        dist = norms[:, None] + col_norms[None, :] - 2.0 * cross
        values = jnp.exp((2.0 * feats - dist) / width)
        rows = row_base + first + jnp.arange(block.shape[0], dtype=jnp.int32)
        return jnp.where(rows[:, None] == col_ids[None, :], jnp.zeros_like(values), values)

    sums = by_blocks(piece, lambda block, first: jnp.sum(kernel_tile(block, first), axis=1))
    own_sums = lax.psum_scatter(sums.reshape(-1), "col", scatter_dimension=0, tiled=True)
    own_density = own_sums / total_pts
    col_density = lax.all_gather(own_density, "row", axis=0, tiled=True)

    def product_tile(block, first):
        weight = kernel_tile(block, first) / col_density[None, :]
        degree = jnp.sum(weight, axis=1)
        numer = jnp.dot(
            weight.astype(jnp.bfloat16), col_vectors, preferred_element_type=jnp.float32
        )
        return (numer, degree)

    numer, degree = by_blocks(piece, product_tile)
    numer = numer.reshape(piece.shape[0], vectors.shape[1])
    numer_own = lax.psum_scatter(numer, "col", scatter_dimension=0, tiled=True)
    degree_own = lax.psum_scatter(
        degree.reshape(-1), "col", scatter_dimension=0, tiled=True
    )
    return (numer_own / degree_own[:, None], jnp.log(own_density))


def augment(pts, first):
    count, feats = pts.shape
    square = pts.astype(jnp.float32)
    square = square * square
    high = square.astype(jnp.bfloat16)
    low = (square - high.astype(jnp.float32)).astype(jnp.bfloat16)
    pair = jnp.concatenate([high, low], axis=1)
    norm = jnp.dot(
        pair, jnp.ones((2 * feats, 128), jnp.bfloat16), preferred_element_type=jnp.float32
    )
    q = 0.5 * feats - 0.5 * norm
    q0 = q.astype(jnp.bfloat16).astype(jnp.float32)
    rest = q - q0
    q1 = rest.astype(jnp.bfloat16).astype(jnp.float32)
    q2 = rest - q1
    lane = lax.broadcasted_iota(jnp.int32, (count, 128), 1)
    other = 3 - first
    extra = jnp.where((lane >= other) & (lane < other + 3), 1.0, 0.0)
    extra = jnp.where(lane == first + 2, q2, extra)
    extra = jnp.where(lane == first + 1, q1, extra)
    extra = jnp.where(lane == first, q0, extra)
    return jnp.concatenate([pts, extra.astype(jnp.bfloat16)], axis=1)


def kernel_body(counts, unit, scale, diagonal, bm, bn, *refs):
    refs = list(refs)
    raw_rows, done_rows, raw_cols, done_cols, before, ahead = [
        [refs.pop(0) for _ in range(count)] for count in counts
    ]
    k_ref, sum_ref = refs.pop(0), refs.pop(0)
    if raw_rows:
        made = refs.pop(0)
        for u, ref in enumerate(raw_rows):
            made[u * unit : (u + 1) * unit, :] = augment(ref[...], 0)
        done_rows = done_rows + [made]
    if raw_cols:
        made = refs.pop(0)
        for u, ref in enumerate(raw_cols):
            made[u * unit : (u + 1) * unit, :] = augment(ref[...], 3)
        done_cols = done_cols + [made]
    skip = 0
    for ref in ahead:
        sum_ref[0:1, skip : skip + ref.shape[1]] = ref[...]
        skip += ref.shape[1]
    c_at = 0
    for col_ref in done_cols:
        for c0 in range(0, col_ref.shape[0], bn):
            total = jnp.zeros((8, bn), jnp.float32)
            r_at = 0
            for row_ref in done_rows:
                for r0 in range(0, row_ref.shape[0], bm):
                    half_log = lax.dot_general(
                        row_ref[r0 : r0 + bm, :],
                        col_ref[c0 : c0 + bn, :],
                        NT,
                        preferred_element_type=jnp.float32,
                    )
                    value = jnp.exp2(half_log * scale)
                    if diagonal and r_at // unit == 0 and c_at // unit == 0:
                        i = lax.broadcasted_iota(jnp.int32, (bm, bn), 0) + r_at
                        j = lax.broadcasted_iota(jnp.int32, (bm, bn), 1) + c_at
                        value = jnp.where(i == j, 0.0, value)
                    k_ref[r_at : r_at + bm, c_at : c_at + bn] = value
                    total = total + jnp.sum(value.reshape(bm // 8, 8, bn), axis=0)
                    r_at += bm
            out = jnp.sum(total, axis=0, keepdims=True)
            at = 0
            for ref in before:
                if at <= c_at < at + ref.shape[1]:
                    out = out + ref[:, c_at - at : c_at - at + bn]
                at += ref.shape[1]
            sum_ref[0:1, skip + c_at : skip + c_at + bn] = out
            c_at += bn


def on_chip(body, shapes, name, limit, *args, scratch=()):
    return pl.pallas_call(
        body,
        out_shape=tuple(shapes),
        in_specs=[VMEM_SPEC] * len(args),
        out_specs=tuple(VMEM_SPEC for _ in shapes),
        scratch_shapes=list(scratch),
        compiler_params=pltpu.CompilerParams(vmem_limit_bytes=limit * MIB),
        name=name,
    )(*args)


def kernel_tile(
    name, raw_rows, done_rows, raw_cols, done_cols, before=(), ahead=(), diagonal=False
):
    groups = [raw_rows, done_rows, raw_cols, done_cols, before, ahead]
    unit, feats = (raw_rows + raw_cols)[0].shape
    wide = feats + 128
    n_rows = unit * len(raw_rows) + sum(x.shape[0] for x in done_rows)
    n_cols = unit * len(raw_cols) + sum(x.shape[0] for x in done_cols)
    scale = 2.0 * math.log2(math.e) / (1.05 * math.sqrt(feats))
    shapes = [
        pltpu.VMEM((n_rows, n_cols), jnp.float32),
        pltpu.VMEM((1, n_cols + sum(x.shape[1] for x in ahead)), jnp.float32),
    ]
    scratch = []
    for raw in (raw_rows, raw_cols):
        if raw:
            made = pltpu.VMEM((len(raw) * unit, wide), jnp.bfloat16)
            (scratch if ahead else shapes).append(made)
    counts = [len(g) for g in groups]
    body = functools.partial(kernel_body, counts, unit, scale, diagonal, 512, 256)
    args = [x for g in groups for x in g]
    return on_chip(body, shapes, name, 12, *args, scratch=scratch)


def own_body(points_ref, vector_ref, row_ref, col_ref, copy_ref):
    row_ref[...] = augment(points_ref[...], 0)
    col_ref[...] = augment(points_ref[...], 3)
    copy_ref[...] = vector_ref[...]


def vectors_body(*refs):
    *vecs, vec_all = refs
    width, unit = vecs[0].shape
    for v, ref in enumerate(vecs):
        vec_all[0:width, v * unit : (v + 1) * unit] = ref[...]
    ones = lax.broadcasted_iota(jnp.int32, (128 - width, len(vecs) * unit), 0) == 0
    vec_all[width:128, :] = jnp.where(ones, 1.0, 0.0).astype(jnp.bfloat16)


def density_body(unit, points_all, sums, inverse_ref, density_ref):
    n_cols = len(sums)
    for v in range(n_cols):
        cols = slice(v * unit, (v + 1) * unit)
        total = sums[0][:, cols]
        for u in range(1, n_cols):
            w = v ^ u
            total = total + sums[u][:, w * unit : (w + 1) * unit]
        density = total / points_all
        if v == 0:
            density_ref[...] = density
        inverse_ref[:, cols] = 1.0 / density


def product(k_refs, firsts, r, bm, inverse_ref, vec_all):
    numer = None
    at = 0
    for k_ref, first in zip(k_refs, firsts):
        cols = slice(at, at + k_ref.shape[1])
        weight = k_ref[first + r : first + r + bm, :] * inverse_ref[:, cols]
        part = lax.dot_general(
            weight.astype(jnp.bfloat16),
            vec_all[:, cols],
            NT,
            preferred_element_type=jnp.float32,
        )
        numer = part if numer is None else numer + part
        at += k_ref.shape[1]
    return numer.T


def give(out_ref, k_refs, firsts, inverse_ref, vec_all, bm):
    width = out_ref.shape[0] - 16
    for r in range(0, out_ref.shape[1], bm):
        numer = product(k_refs, firsts, r, bm, inverse_ref, vec_all)
        degree = numer[width : width + 1, :]
        high = degree.astype(jnp.bfloat16).astype(jnp.float32)
        zero = jnp.zeros((14, bm), jnp.float32)
        tail = jnp.concatenate([high, degree - high, zero], axis=0)
        out_ref[0:width, r : r + bm] = numer[0:width, :].astype(jnp.bfloat16)
        out_ref[width:, r : r + bm] = tail.astype(jnp.bfloat16)


def first_give_body(unit, points_all, first, bm, n_sums, k_near, k_side, vec_all, *refs):
    sums = refs[:n_sums]
    out_ref, inverse_ref, density_ref = refs[n_sums:]
    density_body(unit, points_all, sums, inverse_ref, density_ref)
    give(out_ref, [k_near, k_side], [first, first], inverse_ref, vec_all, bm)


def next_give_body(firsts, bm, *refs):
    *k_refs, vec_all, inverse_ref, out_ref = refs
    give(out_ref, k_refs, firsts, inverse_ref, vec_all, bm)


def keep_body(bm, *refs):
    *k_refs, vec_all, inverse_ref, density_ref, out_ref, log_ref = refs
    height, unit = out_ref.shape
    firsts = [0] * len(k_refs)
    for r in range(0, unit, bm):
        numer = product(k_refs, firsts, r, bm, inverse_ref, vec_all)
        out_ref[:, r : r + bm] = numer[0:height, :]
    log_ref[...] = jnp.log(density_ref[...])


def finish_body(near_ref, *refs):
    *far_refs, out_ref = refs
    width = out_ref.shape[0]
    numer = near_ref[0:width, :]
    degree = near_ref[width : width + 1, :]
    for ref in far_refs:
        far = ref[...].astype(jnp.float32)
        numer = numer + far[0:width, :]
        degree = degree + (far[width : width + 1, :] + far[width + 1 : width + 2, :])
    out_ref[...] = numer / degree


def after(x, *others):
    return lax.optimization_barrier((x, *others))[0]


def grid_device(points, vectors):
    n_col = lax.axis_size("col")
    unit, feats = points.shape
    width = vectors.shape[1]
    points_all = float(unit * n_col * lax.axis_size("row"))
    n_units = n_col // 2

    def across(x, mask):
        return lax.ppermute(x, "col", [(i, i ^ mask) for i in range(n_col)])

    def sibling(x):
        return lax.ppermute(x, "row", [(0, 1), (1, 0)])

    far = across(points, n_units)
    beside = sibling(points)
    augmented = pltpu.VMEM((unit, feats + 128), jnp.bfloat16)
    vec = vectors.T
    row_own, col_own, vec_own = on_chip(
        own_body,
        (augmented, augmented, pltpu.VMEM((width, unit), jnp.bfloat16)),
        "own",
        8,
        points,
        vec,
    )
    held = {0: points}
    bit = n_units // 2
    while bit:
        for u in list(held):
            held[u | bit] = across(held[u], bit)
        bit //= 2
    rows = [held[u] for u in range(1, n_units)]
    far_beside = sibling(after(far, col_own))
    n_wide = 4 * unit

    vec_far = across(after(vec, far), n_units)
    k_near, sums_near, rows_near, cols_near = kernel_tile(
        "near", rows[:-1], [row_own], [beside, far], [col_own], diagonal=True
    )
    k_last, sums_last, row_last = kernel_tile(
        "last", rows[-1:], [], [], [col_own, cols_near], [sums_near]
    )
    k_side, sums = kernel_tile(
        "side", [], [row_own, rows_near, row_last], [far_beside], [], [], [sums_last]
    )
    sums_far = across(sums, n_units)
    all_sums = [sums, sibling(sums), sums_far, sibling(sums_far)]

    vecs = [vec_own, sibling(vec), vec_far, sibling(after(vec_far, sums_far))]
    (vec_all,) = on_chip(
        vectors_body, (pltpu.VMEM((128, n_wide), jnp.bfloat16),), "vectors", 4, *vecs
    )

    packed = pltpu.VMEM((width + 16, unit), jnp.bfloat16)
    away, inverse, density = on_chip(
        functools.partial(first_give_body, unit, points_all, unit, 512, len(all_sums)),
        (
            packed,
            pltpu.VMEM((1, n_wide), jnp.float32),
            pltpu.VMEM((1, unit), jnp.float32),
        ),
        "give_first",
        8,
        k_near,
        k_side,
        vec_all,
        *all_sums,
    )
    back = [across(away, 1)]
    for u in range(2, n_units):
        last = u == n_units - 1
        (away,) = on_chip(
            functools.partial(next_give_body, [0 if last else u * unit, u * unit], 512),
            (packed,),
            "give",
            8,
            k_last if last else k_near,
            k_side,
            vec_all,
            after(inverse, away),
        )
        back.append(across(away, u))
    near, log_density = on_chip(
        functools.partial(keep_body, 512),
        (
            pltpu.VMEM((width + 8, unit), jnp.float32),
            jax.ShapeDtypeStruct((1, unit), jnp.float32),
        ),
        "keep",
        8,
        k_near,
        k_side,
        vec_all,
        inverse,
        density,
    )
    (smoothed,) = on_chip(
        finish_body,
        (jax.ShapeDtypeStruct((width, unit), jnp.float32),),
        "finish",
        8,
        near,
        *back,
    )
    return (smoothed.T, log_density.reshape(unit))


def solution(mesh):
    n_col = mesh.shape["col"]
    n_row = mesh.shape["row"]
    placed = (P(("parts", "row", "col"), None), P(("parts", "row", "col"), None))

    def run(points, vectors):
        unit, feats = points.shape
        paired = n_row == 2 and n_col >= 8 and n_col & (n_col - 1) == 0
        tile_bytes = 4 * (4 * unit) * (n_col // 2 * unit)
        width = vectors.shape[1]
        shaped = unit % 512 == 0 and feats == 128 and width % 16 == 0 and width <= 112
        if paired and shaped and tile_bytes <= 16 * MIB:
            return grid_device(points, vectors)
        return plain_device(points, vectors)

    return jax.shard_map(
        run,
        mesh=mesh,
        in_specs=placed,
        out_specs=(P(("parts", "row", "col"), None), P(("parts", "row", "col"))),
        check_vma=False,
    )
```

```python
import functools
import math

import jax
import jax.numpy as jnp
from jax import lax
from jax.experimental import pallas as pl
from jax.experimental.pallas import tpu as pltpu
from jax.sharding import PartitionSpec as P

MIB = 2**20
NT = (((1,), (1,)), ((), ()))
VMEM_SPEC = pl.BlockSpec(memory_space=pltpu.VMEM)


def by_blocks(piece, tile_fn):
    count = piece.shape[0]
    size = 512
    groups = piece.reshape(count // size, size, piece.shape[1])
    firsts = jnp.arange(count // size, dtype=jnp.int32) * size
    return lax.map(lambda item: tile_fn(item[0], item[1]), (groups, firsts))


def plain_device(points, vectors):
    rows_dev = points.shape[0]
    feats = points.shape[1]
    n_col = lax.axis_size("col")
    n_row = lax.axis_size("row")
    half = rows_dev * n_col
    total_pts = half * n_row
    row_pos = lax.axis_index("row")
    col_pos = lax.axis_index("col")
    width = 1.05 * math.sqrt(feats)
    col_points = lax.all_gather(points, "row", axis=0, tiled=True)
    col_vectors = lax.all_gather(vectors, "row", axis=0, tiled=True)
    local = jnp.arange(n_row * rows_dev, dtype=jnp.int32)
    col_ids = local // rows_dev * half + col_pos * rows_dev + local % rows_dev
    col_norms = jnp.sum(col_points.astype(jnp.float32) ** 2, axis=1)
    row_base = row_pos * half
    piece = lax.all_gather(points, "col", axis=0, tiled=True)

    def kernel_tile(block, first):
        norms = jnp.sum(block.astype(jnp.float32) ** 2, axis=1)
        cross = lax.dot_general(block, col_points, NT, preferred_element_type=jnp.float32)
        dist = norms[:, None] + col_norms[None, :] - 2.0 * cross
        values = jnp.exp((2.0 * feats - dist) / width)
        rows = row_base + first + jnp.arange(block.shape[0], dtype=jnp.int32)
        return jnp.where(rows[:, None] == col_ids[None, :], jnp.zeros_like(values), values)

    sums = by_blocks(piece, lambda block, first: jnp.sum(kernel_tile(block, first), axis=1))
    own_sums = lax.psum_scatter(sums.reshape(-1), "col", scatter_dimension=0, tiled=True)
    own_density = own_sums / total_pts
    col_density = lax.all_gather(own_density, "row", axis=0, tiled=True)

    def product_tile(block, first):
        weight = kernel_tile(block, first) / col_density[None, :]
        degree = jnp.sum(weight, axis=1)
        numer = jnp.dot(
            weight.astype(jnp.bfloat16), col_vectors, preferred_element_type=jnp.float32
        )
        return (numer, degree)

    numer, degree = by_blocks(piece, product_tile)
    numer = numer.reshape(piece.shape[0], vectors.shape[1])
    numer_own = lax.psum_scatter(numer, "col", scatter_dimension=0, tiled=True)
    degree_own = lax.psum_scatter(
        degree.reshape(-1), "col", scatter_dimension=0, tiled=True
    )
    return (numer_own / degree_own[:, None], jnp.log(own_density))


def augment(pts, first):
    count, feats = pts.shape
    square = pts.astype(jnp.float32)
    square = square * square
    high = square.astype(jnp.bfloat16)
    low = (square - high.astype(jnp.float32)).astype(jnp.bfloat16)
    pair = jnp.concatenate([high, low], axis=1)
    norm = jnp.dot(
        pair, jnp.ones((2 * feats, 128), jnp.bfloat16), preferred_element_type=jnp.float32
    )
    q = 0.5 * feats - 0.5 * norm
    q0 = q.astype(jnp.bfloat16).astype(jnp.float32)
    rest = q - q0
    q1 = rest.astype(jnp.bfloat16).astype(jnp.float32)
    q2 = rest - q1
    lane = lax.broadcasted_iota(jnp.int32, (count, 128), 1)
    other = 3 - first
    extra = jnp.where((lane >= other) & (lane < other + 3), 1.0, 0.0)
    extra = jnp.where(lane == first + 2, q2, extra)
    extra = jnp.where(lane == first + 1, q1, extra)
    extra = jnp.where(lane == first, q0, extra)
    return jnp.concatenate([pts, extra.astype(jnp.bfloat16)], axis=1)


def kernel_body(counts, unit, scale, diagonal, bm, bn, *refs):
    refs = list(refs)
    raw_rows, done_rows, raw_cols, done_cols, before, ahead = [
        [refs.pop(0) for _ in range(count)] for count in counts
    ]
    k_ref, sum_ref = refs.pop(0), refs.pop(0)
    if raw_rows:
        made = refs.pop(0)
        for u, ref in enumerate(raw_rows):
            made[u * unit : (u + 1) * unit, :] = augment(ref[...], 0)
        done_rows = done_rows + [made]
    if raw_cols:
        made = refs.pop(0)
        for u, ref in enumerate(raw_cols):
            made[u * unit : (u + 1) * unit, :] = augment(ref[...], 3)
        done_cols = done_cols + [made]
    skip = 0
    for ref in ahead:
        sum_ref[0:1, skip : skip + ref.shape[1]] = ref[...]
        skip += ref.shape[1]
    c_at = 0
    for col_ref in done_cols:
        for c0 in range(0, col_ref.shape[0], bn):
            total = jnp.zeros((8, bn), jnp.float32)
            r_at = 0
            for row_ref in done_rows:
                for r0 in range(0, row_ref.shape[0], bm):
                    half_log = lax.dot_general(
                        row_ref[r0 : r0 + bm, :],
                        col_ref[c0 : c0 + bn, :],
                        NT,
                        preferred_element_type=jnp.float32,
                    )
                    value = jnp.exp2(half_log * scale)
                    if diagonal and r_at // unit == 0 and c_at // unit == 0:
                        i = lax.broadcasted_iota(jnp.int32, (bm, bn), 0) + r_at
                        j = lax.broadcasted_iota(jnp.int32, (bm, bn), 1) + c_at
                        value = jnp.where(i == j, 0.0, value)
                    k_ref[r_at : r_at + bm, c_at : c_at + bn] = value
                    total = total + jnp.sum(value.reshape(bm // 8, 8, bn), axis=0)
                    r_at += bm
            out = jnp.sum(total, axis=0, keepdims=True)
            at = 0
            for ref in before:
                if at <= c_at < at + ref.shape[1]:
                    out = out + ref[:, c_at - at : c_at - at + bn]
                at += ref.shape[1]
            sum_ref[0:1, skip + c_at : skip + c_at + bn] = out
            c_at += bn


def on_chip(body, shapes, name, limit, *args, scratch=()):
    return pl.pallas_call(
        body,
        out_shape=tuple(shapes),
        in_specs=[VMEM_SPEC] * len(args),
        out_specs=tuple(VMEM_SPEC for _ in shapes),
        scratch_shapes=list(scratch),
        compiler_params=pltpu.CompilerParams(vmem_limit_bytes=limit * MIB),
        name=name,
    )(*args)


def kernel_tile(
    name, raw_rows, done_rows, raw_cols, done_cols, before=(), ahead=(), diagonal=False
):
    groups = [raw_rows, done_rows, raw_cols, done_cols, before, ahead]
    unit, feats = (raw_rows + raw_cols)[0].shape
    wide = feats + 128
    n_rows = unit * len(raw_rows) + sum(x.shape[0] for x in done_rows)
    n_cols = unit * len(raw_cols) + sum(x.shape[0] for x in done_cols)
    scale = 2.0 * math.log2(math.e) / (1.05 * math.sqrt(feats))
    shapes = [
        pltpu.VMEM((n_rows, n_cols), jnp.float32),
        pltpu.VMEM((1, n_cols + sum(x.shape[1] for x in ahead)), jnp.float32),
    ]
    scratch = []
    for raw in (raw_rows, raw_cols):
        if raw:
            made = pltpu.VMEM((len(raw) * unit, wide), jnp.bfloat16)
            (scratch if ahead else shapes).append(made)
    counts = [len(g) for g in groups]
    body = functools.partial(kernel_body, counts, unit, scale, diagonal, 512, 256)
    args = [x for g in groups for x in g]
    return on_chip(body, shapes, name, 12, *args, scratch=scratch)


def own_body(points_ref, vector_ref, row_ref, col_ref, copy_ref):
    row_ref[...] = augment(points_ref[...], 0)
    col_ref[...] = augment(points_ref[...], 3)
    copy_ref[...] = vector_ref[...]


def vectors_body(*refs):
    *vecs, vec_all = refs
    width, unit = vecs[0].shape
    for v, ref in enumerate(vecs):
        vec_all[0:width, v * unit : (v + 1) * unit] = ref[...]
    ones = lax.broadcasted_iota(jnp.int32, (128 - width, len(vecs) * unit), 0) == 0
    vec_all[width:128, :] = jnp.where(ones, 1.0, 0.0).astype(jnp.bfloat16)


def density_body(unit, points_all, sums, inverse_ref, density_ref):
    n_cols = len(sums)
    for v in range(n_cols):
        cols = slice(v * unit, (v + 1) * unit)
        total = sums[0][:, cols]
        for u in range(1, n_cols):
            w = v ^ u
            total = total + sums[u][:, w * unit : (w + 1) * unit]
        density = total / points_all
        if v == 0:
            density_ref[...] = density
        inverse_ref[:, cols] = 1.0 / density


def product(k_refs, firsts, r, bm, inverse_ref, vec_all):
    numer = None
    at = 0
    for k_ref, first in zip(k_refs, firsts):
        cols = slice(at, at + k_ref.shape[1])
        weight = k_ref[first + r : first + r + bm, :] * inverse_ref[:, cols]
        part = lax.dot_general(
            weight.astype(jnp.bfloat16),
            vec_all[:, cols],
            NT,
            preferred_element_type=jnp.float32,
        )
        numer = part if numer is None else numer + part
        at += k_ref.shape[1]
    return numer.T


def give(out_ref, k_refs, firsts, inverse_ref, vec_all, bm):
    width = out_ref.shape[0] - 16
    for r in range(0, out_ref.shape[1], bm):
        numer = product(k_refs, firsts, r, bm, inverse_ref, vec_all)
        degree = numer[width : width + 1, :]
        high = degree.astype(jnp.bfloat16).astype(jnp.float32)
        zero = jnp.zeros((14, bm), jnp.float32)
        tail = jnp.concatenate([high, degree - high, zero], axis=0)
        out_ref[0:width, r : r + bm] = numer[0:width, :].astype(jnp.bfloat16)
        out_ref[width:, r : r + bm] = tail.astype(jnp.bfloat16)


def give_body(unit, points_all, bm, n_sums, k_near, k_last, k_side, vec_all, *refs):
    sums = refs[:n_sums]
    *outs, inverse_ref, density_ref = refs[n_sums:]
    density_body(unit, points_all, sums, inverse_ref, density_ref)
    for u, out_ref in enumerate(outs, 1):
        last = u == len(outs)
        k_refs = [k_last if last else k_near, k_side]
        firsts = [0 if last else u * unit, u * unit]
        give(out_ref, k_refs, firsts, inverse_ref, vec_all, bm)


def keep_body(bm, *refs):
    *k_refs, vec_all, inverse_ref, density_ref, out_ref, log_ref = refs
    height, unit = out_ref.shape
    firsts = [0] * len(k_refs)
    for r in range(0, unit, bm):
        numer = product(k_refs, firsts, r, bm, inverse_ref, vec_all)
        out_ref[:, r : r + bm] = numer[0:height, :]
    log_ref[...] = jnp.log(density_ref[...])


def finish_body(near_ref, *refs):
    *far_refs, out_ref = refs
    width = out_ref.shape[0]
    numer = near_ref[0:width, :]
    degree = near_ref[width : width + 1, :]
    for ref in far_refs:
        far = ref[...].astype(jnp.float32)
        numer = numer + far[0:width, :]
        degree = degree + (far[width : width + 1, :] + far[width + 1 : width + 2, :])
    out_ref[...] = numer / degree


def after(x, *others):
    return lax.optimization_barrier((x, *others))[0]


def grid_device(points, vectors):
    n_col = lax.axis_size("col")
    unit, feats = points.shape
    width = vectors.shape[1]
    points_all = float(unit * n_col * lax.axis_size("row"))
    n_units = n_col // 2

    def across(x, mask):
        return lax.ppermute(x, "col", [(i, i ^ mask) for i in range(n_col)])

    def sibling(x):
        return lax.ppermute(x, "row", [(0, 1), (1, 0)])

    far = across(points, n_units)
    beside = sibling(points)
    augmented = pltpu.VMEM((unit, feats + 128), jnp.bfloat16)
    vec = vectors.T
    row_own, col_own, vec_own = on_chip(
        own_body,
        (augmented, augmented, pltpu.VMEM((width, unit), jnp.bfloat16)),
        "own",
        8,
        points,
        vec,
    )
    held = {0: points}
    bit = n_units // 2
    while bit:
        for u in list(held):
            held[u | bit] = across(held[u], bit)
        bit //= 2
    rows = [held[u] for u in range(1, n_units)]
    far_beside = sibling(after(far, col_own))
    n_wide = 4 * unit

    vec_far = across(after(vec, far), n_units)
    k_near, sums_near, rows_near, cols_near = kernel_tile(
        "near", rows[:-1], [row_own], [beside, far], [col_own], diagonal=True
    )
    k_last, sums_last, row_last = kernel_tile(
        "last", rows[-1:], [], [], [col_own, cols_near], [sums_near]
    )
    k_side, sums = kernel_tile(
        "side", [], [row_own, rows_near, row_last], [far_beside], [], [], [sums_last]
    )
    sums_far = across(sums, n_units)
    all_sums = [sums, sibling(sums), sums_far, sibling(sums_far)]

    vecs = [vec_own, sibling(vec), vec_far, sibling(after(vec_far, sums_far))]
    (vec_all,) = on_chip(
        vectors_body, (pltpu.VMEM((128, n_wide), jnp.bfloat16),), "vectors", 4, *vecs
    )

    packed = pltpu.VMEM((width + 16, unit), jnp.bfloat16)
    *away, inverse, density = on_chip(
        functools.partial(give_body, unit, points_all, 512, len(all_sums)),
        (packed,) * (n_units - 1)
        + (pltpu.VMEM((1, n_wide), jnp.float32), pltpu.VMEM((1, unit), jnp.float32)),
        "give",
        8,
        k_near,
        k_last,
        k_side,
        vec_all,
        *all_sums,
    )
    back = [across(x, u) for u, x in enumerate(away, 1)]
    near, log_density = on_chip(
        functools.partial(keep_body, 512),
        (
            pltpu.VMEM((width + 8, unit), jnp.float32),
            jax.ShapeDtypeStruct((1, unit), jnp.float32),
        ),
        "keep",
        8,
        k_near,
        k_side,
        vec_all,
        inverse,
        density,
    )
    (smoothed,) = on_chip(
        finish_body,
        (jax.ShapeDtypeStruct((width, unit), jnp.float32),),
        "finish",
        8,
        near,
        *back[::-1],
    )
    return (smoothed.T, log_density.reshape(unit))


def solution(mesh):
    n_col = mesh.shape["col"]
    n_row = mesh.shape["row"]
    placed = (P(("parts", "row", "col"), None), P(("parts", "row", "col"), None))

    def run(points, vectors):
        unit, feats = points.shape
        paired = n_row == 2 and n_col >= 8 and n_col & (n_col - 1) == 0
        tile_bytes = 4 * (4 * unit) * (n_col // 2 * unit)
        width = vectors.shape[1]
        shaped = unit % 512 == 0 and feats == 128 and width % 16 == 0 and width <= 112
        if paired and shaped and tile_bytes <= 16 * MIB:
            return grid_device(points, vectors)
        return plain_device(points, vectors)

    return jax.shard_map(
        run,
        mesh=mesh,
        in_specs=placed,
        out_specs=(P(("parts", "row", "col"), None), P(("parts", "row", "col"))),
        check_vma=False,
    )
```

```python
import functools
import math

import jax
import jax.numpy as jnp
from jax import lax
from jax.experimental import pallas as pl
from jax.experimental.pallas import tpu as pltpu
from jax.sharding import PartitionSpec as P

MIB = 2**20
NT = (((1,), (1,)), ((), ()))
VMEM_SPEC = pl.BlockSpec(memory_space=pltpu.VMEM)


def by_blocks(piece, tile_fn):
    count = piece.shape[0]
    size = 512
    groups = piece.reshape(count // size, size, piece.shape[1])
    firsts = jnp.arange(count // size, dtype=jnp.int32) * size
    return lax.map(lambda item: tile_fn(item[0], item[1]), (groups, firsts))


def plain_device(points, vectors):
    rows_dev = points.shape[0]
    feats = points.shape[1]
    n_col = lax.axis_size("col")
    n_row = lax.axis_size("row")
    half = rows_dev * n_col
    total_pts = half * n_row
    row_pos = lax.axis_index("row")
    col_pos = lax.axis_index("col")
    width = 1.05 * math.sqrt(feats)
    col_points = lax.all_gather(points, "row", axis=0, tiled=True)
    col_vectors = lax.all_gather(vectors, "row", axis=0, tiled=True)
    local = jnp.arange(n_row * rows_dev, dtype=jnp.int32)
    col_ids = local // rows_dev * half + col_pos * rows_dev + local % rows_dev
    col_norms = jnp.sum(col_points.astype(jnp.float32) ** 2, axis=1)
    row_base = row_pos * half
    piece = lax.all_gather(points, "col", axis=0, tiled=True)

    def kernel_tile(block, first):
        norms = jnp.sum(block.astype(jnp.float32) ** 2, axis=1)
        cross = lax.dot_general(block, col_points, NT, preferred_element_type=jnp.float32)
        dist = norms[:, None] + col_norms[None, :] - 2.0 * cross
        values = jnp.exp((2.0 * feats - dist) / width)
        rows = row_base + first + jnp.arange(block.shape[0], dtype=jnp.int32)
        return jnp.where(rows[:, None] == col_ids[None, :], jnp.zeros_like(values), values)

    sums = by_blocks(piece, lambda block, first: jnp.sum(kernel_tile(block, first), axis=1))
    own_sums = lax.psum_scatter(sums.reshape(-1), "col", scatter_dimension=0, tiled=True)
    own_density = own_sums / total_pts
    col_density = lax.all_gather(own_density, "row", axis=0, tiled=True)

    def product_tile(block, first):
        weight = kernel_tile(block, first) / col_density[None, :]
        degree = jnp.sum(weight, axis=1)
        numer = jnp.dot(
            weight.astype(jnp.bfloat16), col_vectors, preferred_element_type=jnp.float32
        )
        return (numer, degree)

    numer, degree = by_blocks(piece, product_tile)
    numer = numer.reshape(piece.shape[0], vectors.shape[1])
    numer_own = lax.psum_scatter(numer, "col", scatter_dimension=0, tiled=True)
    degree_own = lax.psum_scatter(
        degree.reshape(-1), "col", scatter_dimension=0, tiled=True
    )
    return (numer_own / degree_own[:, None], jnp.log(own_density))


def augment(pts, first):
    count, feats = pts.shape
    square = pts.astype(jnp.float32)
    square = square * square
    high = square.astype(jnp.bfloat16)
    low = (square - high.astype(jnp.float32)).astype(jnp.bfloat16)
    pair = jnp.concatenate([high, low], axis=1)
    norm = jnp.dot(
        pair, jnp.ones((2 * feats, 128), jnp.bfloat16), preferred_element_type=jnp.float32
    )
    q = 0.5 * feats - 0.5 * norm
    q0 = q.astype(jnp.bfloat16).astype(jnp.float32)
    rest = q - q0
    q1 = rest.astype(jnp.bfloat16).astype(jnp.float32)
    q2 = rest - q1
    lane = lax.broadcasted_iota(jnp.int32, (count, 128), 1)
    other = 3 - first
    extra = jnp.where((lane >= other) & (lane < other + 3), 1.0, 0.0)
    extra = jnp.where(lane == first + 2, q2, extra)
    extra = jnp.where(lane == first + 1, q1, extra)
    extra = jnp.where(lane == first, q0, extra)
    return jnp.concatenate([pts, extra.astype(jnp.bfloat16)], axis=1)


def kernel_body(counts, unit, scale, diagonal, bm, bn, *refs):
    refs = list(refs)
    raw_rows, done_rows, raw_cols, done_cols, before, ahead = [
        [refs.pop(0) for _ in range(count)] for count in counts
    ]
    k_ref, sum_ref = refs.pop(0), refs.pop(0)
    if raw_rows:
        made = refs.pop(0)
        for u, ref in enumerate(raw_rows):
            made[u * unit : (u + 1) * unit, :] = augment(ref[...], 0)
        done_rows = done_rows + [made]
    if raw_cols:
        made = refs.pop(0)
        for u, ref in enumerate(raw_cols):
            made[u * unit : (u + 1) * unit, :] = augment(ref[...], 3)
        done_cols = done_cols + [made]
    skip = 0
    for ref in ahead:
        sum_ref[0:1, skip : skip + ref.shape[1]] = ref[...]
        skip += ref.shape[1]
    c_at = 0
    for col_ref in done_cols:
        for c0 in range(0, col_ref.shape[0], bn):
            total = jnp.zeros((8, bn), jnp.float32)
            r_at = 0
            for row_ref in done_rows:
                for r0 in range(0, row_ref.shape[0], bm):
                    half_log = lax.dot_general(
                        row_ref[r0 : r0 + bm, :],
                        col_ref[c0 : c0 + bn, :],
                        NT,
                        preferred_element_type=jnp.float32,
                    )
                    value = jnp.exp2(half_log * scale)
                    if diagonal and r_at // unit == 0 and c_at // unit == 0:
                        i = lax.broadcasted_iota(jnp.int32, (bm, bn), 0) + r_at
                        j = lax.broadcasted_iota(jnp.int32, (bm, bn), 1) + c_at
                        value = jnp.where(i == j, 0.0, value)
                    k_ref[r_at : r_at + bm, c_at : c_at + bn] = value
                    total = total + jnp.sum(value.reshape(bm // 8, 8, bn), axis=0)
                    r_at += bm
            out = jnp.sum(total, axis=0, keepdims=True)
            at = 0
            for ref in before:
                if at <= c_at < at + ref.shape[1]:
                    out = out + ref[:, c_at - at : c_at - at + bn]
                at += ref.shape[1]
            sum_ref[0:1, skip + c_at : skip + c_at + bn] = out
            c_at += bn


def last_body(unit, scale, *refs):
    row_ref, col_own, cols_near, before, row_own, rows_near, col_ref = refs[:7]
    k_last, k_side, sum_ref, early, row_made, col_made = refs[7:]
    first = (row_ref, col_own, cols_near, before, k_last, early, row_made)
    kernel_body([1, 0, 0, 2, 1, 0], unit, scale, False, 512, 256, *first)
    second = (row_own, rows_near, row_made, col_ref, early, k_side, sum_ref, col_made)
    kernel_body([0, 3, 1, 0, 0, 1], unit, scale, False, 512, 256, *second)


def on_chip(body, shapes, name, limit, *args, scratch=()):
    return pl.pallas_call(
        body,
        out_shape=tuple(shapes),
        in_specs=[VMEM_SPEC] * len(args),
        out_specs=tuple(VMEM_SPEC for _ in shapes),
        scratch_shapes=list(scratch),
        compiler_params=pltpu.CompilerParams(vmem_limit_bytes=limit * MIB),
        name=name,
    )(*args)


def kernel_tile(
    name, raw_rows, done_rows, raw_cols, done_cols, before=(), ahead=(), diagonal=False
):
    groups = [raw_rows, done_rows, raw_cols, done_cols, before, ahead]
    unit, feats = (raw_rows + raw_cols)[0].shape
    wide = feats + 128
    n_rows = unit * len(raw_rows) + sum(x.shape[0] for x in done_rows)
    n_cols = unit * len(raw_cols) + sum(x.shape[0] for x in done_cols)
    scale = 2.0 * math.log2(math.e) / (1.05 * math.sqrt(feats))
    shapes = [
        pltpu.VMEM((n_rows, n_cols), jnp.float32),
        pltpu.VMEM((1, n_cols + sum(x.shape[1] for x in ahead)), jnp.float32),
    ]
    scratch = []
    for raw in (raw_rows, raw_cols):
        if raw:
            made = pltpu.VMEM((len(raw) * unit, wide), jnp.bfloat16)
            (scratch if ahead else shapes).append(made)
    counts = [len(g) for g in groups]
    body = functools.partial(kernel_body, counts, unit, scale, diagonal, 512, 256)
    args = [x for g in groups for x in g]
    return on_chip(body, shapes, name, 12, *args, scratch=scratch)


def own_body(points_ref, vector_ref, row_ref, col_ref, copy_ref):
    row_ref[...] = augment(points_ref[...], 0)
    col_ref[...] = augment(points_ref[...], 3)
    copy_ref[...] = vector_ref[...]


def vectors_body(*refs):
    *vecs, vec_all = refs
    width, unit = vecs[0].shape
    for v, ref in enumerate(vecs):
        vec_all[0:width, v * unit : (v + 1) * unit] = ref[...]
    ones = lax.broadcasted_iota(jnp.int32, (128 - width, len(vecs) * unit), 0) == 0
    vec_all[width:128, :] = jnp.where(ones, 1.0, 0.0).astype(jnp.bfloat16)


def density_body(unit, points_all, sums, inverse_ref, density_ref):
    n_cols = len(sums)
    for v in range(n_cols):
        cols = slice(v * unit, (v + 1) * unit)
        total = sums[0][:, cols]
        for u in range(1, n_cols):
            w = v ^ u
            total = total + sums[u][:, w * unit : (w + 1) * unit]
        density = total / points_all
        if v == 0:
            density_ref[...] = density
        inverse_ref[:, cols] = 1.0 / density


def product(k_refs, firsts, r, bm, inverse_ref, vec_all):
    numer = None
    at = 0
    for k_ref, first in zip(k_refs, firsts):
        cols = slice(at, at + k_ref.shape[1])
        weight = k_ref[first + r : first + r + bm, :] * inverse_ref[:, cols]
        part = lax.dot_general(
            weight.astype(jnp.bfloat16),
            vec_all[:, cols],
            NT,
            preferred_element_type=jnp.float32,
        )
        numer = part if numer is None else numer + part
        at += k_ref.shape[1]
    return numer.T


def give(out_ref, k_refs, firsts, inverse_ref, vec_all, bm):
    width = out_ref.shape[0] - 16
    for r in range(0, out_ref.shape[1], bm):
        numer = product(k_refs, firsts, r, bm, inverse_ref, vec_all)
        degree = numer[width : width + 1, :]
        high = degree.astype(jnp.bfloat16).astype(jnp.float32)
        zero = jnp.zeros((14, bm), jnp.float32)
        tail = jnp.concatenate([high, degree - high, zero], axis=0)
        out_ref[0:width, r : r + bm] = numer[0:width, :].astype(jnp.bfloat16)
        out_ref[width:, r : r + bm] = tail.astype(jnp.bfloat16)


def give_body(unit, points_all, bm, n_sums, k_near, k_last, k_side, vec_all, *refs):
    sums = refs[:n_sums]
    *outs, inverse_ref, density_ref = refs[n_sums:]
    density_body(unit, points_all, sums, inverse_ref, density_ref)
    for u, out_ref in enumerate(outs, 1):
        last = u == len(outs)
        k_refs = [k_last if last else k_near, k_side]
        firsts = [0 if last else u * unit, u * unit]
        give(out_ref, k_refs, firsts, inverse_ref, vec_all, bm)


def keep_body(bm, *refs):
    *k_refs, vec_all, inverse_ref, density_ref, out_ref, log_ref = refs
    height, unit = out_ref.shape
    firsts = [0] * len(k_refs)
    for r in range(0, unit, bm):
        numer = product(k_refs, firsts, r, bm, inverse_ref, vec_all)
        out_ref[:, r : r + bm] = numer[0:height, :]
    log_ref[...] = jnp.log(density_ref[...])


def finish_body(near_ref, *refs):
    *far_refs, out_ref = refs
    width = out_ref.shape[0]
    numer = near_ref[0:width, :]
    degree = near_ref[width : width + 1, :]
    for ref in far_refs:
        far = ref[...].astype(jnp.float32)
        numer = numer + far[0:width, :]
        degree = degree + (far[width : width + 1, :] + far[width + 1 : width + 2, :])
    out_ref[...] = numer / degree


def after(x, *others):
    return lax.optimization_barrier((x, *others))[0]


def grid_device(points, vectors):
    n_col = lax.axis_size("col")
    unit, feats = points.shape
    width = vectors.shape[1]
    points_all = float(unit * n_col * lax.axis_size("row"))
    n_units = n_col // 2

    def across(x, mask):
        return lax.ppermute(x, "col", [(i, i ^ mask) for i in range(n_col)])

    def sibling(x):
        return lax.ppermute(x, "row", [(0, 1), (1, 0)])

    far = across(points, n_units)
    beside = sibling(points)
    augmented = pltpu.VMEM((unit, feats + 128), jnp.bfloat16)
    vec = vectors.T
    row_own, col_own, vec_own = on_chip(
        own_body,
        (augmented, augmented, pltpu.VMEM((width, unit), jnp.bfloat16)),
        "own",
        8,
        points,
        vec,
    )
    held = {0: points}
    bit = n_units // 2
    while bit:
        for u in list(held):
            held[u | bit] = across(held[u], bit)
        bit //= 2
    rows = [held[u] for u in range(1, n_units)]
    far_beside = sibling(after(far, col_own))
    n_wide = 4 * unit

    vec_far = across(after(vec, far), n_units)
    k_near, sums_near, rows_near, cols_near = kernel_tile(
        "near", rows[:-1], [row_own], [beside, far], [col_own], diagonal=True
    )
    scale = 2.0 * math.log2(math.e) / (1.05 * math.sqrt(feats))
    n_rows = n_units * unit
    k_last, k_side, sums = on_chip(
        functools.partial(last_body, unit, scale),
        (
            pltpu.VMEM((unit, 3 * unit), jnp.float32),
            pltpu.VMEM((n_rows, unit), jnp.float32),
            pltpu.VMEM((1, n_wide), jnp.float32),
        ),
        "last",
        12,
        rows[-1],
        col_own,
        cols_near,
        sums_near,
        row_own,
        rows_near,
        far_beside,
        scratch=(pltpu.VMEM((1, 3 * unit), jnp.float32), augmented, augmented),
    )
    sums_far = across(sums, n_units)
    all_sums = [sums, sibling(sums), sums_far, sibling(sums_far)]

    vecs = [vec_own, sibling(vec), vec_far, sibling(after(vec_far, sums_far))]
    (vec_all,) = on_chip(
        vectors_body, (pltpu.VMEM((128, n_wide), jnp.bfloat16),), "vectors", 4, *vecs
    )

    packed = pltpu.VMEM((width + 16, unit), jnp.bfloat16)
    *away, inverse, density = on_chip(
        functools.partial(give_body, unit, points_all, 512, len(all_sums)),
        (packed,) * (n_units - 1)
        + (pltpu.VMEM((1, n_wide), jnp.float32), pltpu.VMEM((1, unit), jnp.float32)),
        "give",
        8,
        k_near,
        k_last,
        k_side,
        vec_all,
        *all_sums,
    )
    back = [across(x, u) for u, x in enumerate(away, 1)]
    near, log_density = on_chip(
        functools.partial(keep_body, 512),
        (
            pltpu.VMEM((width + 8, unit), jnp.float32),
            jax.ShapeDtypeStruct((1, unit), jnp.float32),
        ),
        "keep",
        8,
        k_near,
        k_side,
        vec_all,
        inverse,
        density,
    )
    (smoothed,) = on_chip(
        finish_body,
        (jax.ShapeDtypeStruct((width, unit), jnp.float32),),
        "finish",
        8,
        near,
        *back[::-1],
    )
    return (smoothed.T, log_density.reshape(unit))


def solution(mesh):
    n_col = mesh.shape["col"]
    n_row = mesh.shape["row"]
    placed = (P(("parts", "row", "col"), None), P(("parts", "row", "col"), None))

    def run(points, vectors):
        unit, feats = points.shape
        paired = n_row == 2 and n_col >= 8 and n_col & (n_col - 1) == 0
        tile_bytes = 4 * (4 * unit) * (n_col // 2 * unit)
        width = vectors.shape[1]
        shaped = unit % 512 == 0 and feats == 128 and width % 16 == 0 and width <= 112
        if paired and shaped and tile_bytes <= 16 * MIB:
            return grid_device(points, vectors)
        return plain_device(points, vectors)

    return jax.shard_map(
        run,
        mesh=mesh,
        in_specs=placed,
        out_specs=(P(("parts", "row", "col"), None), P(("parts", "row", "col"))),
        check_vma=False,
    )
```
